256 devices in a mesh: frame: 8 (over x_lo, y), patch: 32 (over z, x_hi, core).
Axes of the slice: x: 4 (x_hi: 2, x_lo: 2; x = x_hi * 2 + x_lo), y: 4, z: 8, core: 2. Of those that a mesh axis runs over, the one named last changes fastest.
Arguments:
- latent: bfloat16 [16, 64, 112, 320], P('frame', 'patch'), may hold values from -24 to 24
- timestep: int32 [1], replicated, may hold values from 0 to 24
- time_weight: bfloat16 [320, 320], replicated, may hold values from -0.3125 to 0.3125
- norm_gain: float32 [320], replicated, may hold values from 0.1 to 1.9
- norm_bias: float32 [320], replicated, may hold values from -3 to 3
- spatial_qkv: bfloat16 [320, 960], replicated, may hold values from -2 to 2
- spatial_out: bfloat16 [320, 320], replicated, may hold values from -0.3125 to 0.3125
- stale_codes: bfloat16 [16, 64, 112, 320], P('frame', 'patch'), may hold values from -8 to 8
- stale_exponents: int32 [16, 64, 5], P('frame', 'patch'), may hold values from -1 to 2
- temporal_qkv: bfloat16 [320, 960], replicated, may hold values from -2 to 2
- temporal_out: bfloat16 [320, 320], replicated, may hold values from -0.3125 to 0.3125
Outputs:
- block_output: bfloat16 [16, 64, 112, 320], P('frame', 'patch')
- residual_codes: bfloat16 [16, 64, 112, 320], P('frame', 'patch')
The draws below stay inside these ranges and needn't reach their ends.
All inputs are finite; a program needn't handle non-finite values.
Results may differ from the reference program's by a relative error of at most 0.02.
The reference program's roundings to bfloat16 on the way count: a program that leaves them out, or rounds other values in their place, can miss the bound.
Values may be sent and summed in bfloat16 or wider, within the bound.
A program may use at most 128 MiB of HBM per device.

```python
import math
import jax
import jax.numpy as jnp
from jax import lax

C = 320
HEAD = 64
GROUPS = 32
W = 112
ROWS_DEV = 2
FRAMES = 16
ROWS = 64


def draw_latent(key, part):
    key = jax.random.fold_in(key, 11)
    position = jnp.arange(ROWS, dtype=jnp.float32) / max(ROWS - 1, 1)
    values = jax.random.normal(key, (FRAMES, ROWS, W, C), jnp.float32)
    values = values * (1.0 + 2.0 * position)[None, :, None, None] + (0.5 + 2.5 * position)[None, :, None, None]
    return jnp.clip(values, -24.0, 24.0).astype(jnp.bfloat16)


def draw_stale_codes(key, part):
    key = jax.random.fold_in(key, 23)
    values = jax.random.normal(key, (FRAMES, ROWS, W, C), jnp.float32)
    return jnp.clip(values, -8.0, 8.0).astype(jnp.bfloat16)


def draw_spatial_qkv(key, part):
    key = jax.random.fold_in(key, 37)
    values = jax.random.normal(key, (C, 3 * C), jnp.float32) * C ** (-0.5)
    return jnp.clip(values, -2.0, 2.0).astype(jnp.bfloat16)


def draw_temporal_qkv(key, part):
    key = jax.random.fold_in(key, 41)
    values = jax.random.normal(key, (C, 3 * C), jnp.float32) * C ** (-0.5)
    return jnp.clip(values, -2.0, 2.0).astype(jnp.bfloat16)


def place_ends(array, own_key, least, high):
    index_at = [jax.random.randint(jax.random.fold_in(own_key, axis), (), 0, length) for axis, length in enumerate(array.shape)]
    main_axis = array.shape.index(max(array.shape))
    neighbour = index_at[:main_axis] + [(index_at[main_axis] + 1) % array.shape[main_axis]] + index_at[main_axis + 1:]
    return array.at[tuple(index_at)].set(least).at[tuple(neighbour)].set(high)


def gaussian(own_key, extent, scale, reach, kind=jnp.bfloat16):
    entries = jax.random.normal(own_key, extent, jnp.float32) * scale
    return jnp.minimum(jnp.maximum(entries, -reach), reach).astype(kind)


def setup_inputs(seed: int = 0) -> dict:
    arg_keys = jax.random.split(jax.random.key(seed), 12)
    latent = draw_latent(jax.random.fold_in(arg_keys[11], 71), 0)
    timestep = jax.random.randint(arg_keys[1], (1,), 0, 25).astype(jnp.int32)
    time_weight = gaussian(arg_keys[2], (C, C), C ** -0.5, 0.3125)
    norm_gain = jnp.clip(1.0 + 0.18 * jax.random.normal(arg_keys[3], (C,), jnp.float32), 0.1, 1.9)
    norm_bias = gaussian(arg_keys[4], (C,), 0.5, 3.0, jnp.float32)
    spatial_qkv = draw_spatial_qkv(jax.random.fold_in(arg_keys[11], 71), 0)
    spatial_out = gaussian(arg_keys[6], (C, C), C ** -0.5, 0.3125)
    stale_codes = draw_stale_codes(jax.random.fold_in(arg_keys[11], 71), 0)
    stale_exponents = place_ends(jax.random.randint(arg_keys[8], (FRAMES, ROWS, C // HEAD), -1, 3), jax.random.fold_in(arg_keys[8], 1), -1, 2).astype(jnp.int32)
    temporal_qkv = draw_temporal_qkv(jax.random.fold_in(arg_keys[11], 71), 0)
    temporal_out = gaussian(arg_keys[10], (C, C), C ** -0.5, 0.3125)
    return {"latent": latent, "timestep": timestep, "time_weight": time_weight, "norm_gain": norm_gain, "norm_bias": norm_bias, "spatial_qkv": spatial_qkv, "spatial_out": spatial_out, "stale_codes": stale_codes, "stale_exponents": stale_exponents, "temporal_qkv": temporal_qkv, "temporal_out": temporal_out}


def sinusoid(position, channels):
    half_width = channels // 2
    frequency = jnp.exp(-math.log(10000.0) * jnp.arange(half_width, dtype=jnp.float32) / half_width)
    angles = position[..., None] * frequency
    return jnp.concatenate([jnp.cos(angles), jnp.sin(angles)], axis=-1)

def reference(latent, timestep, time_weight, norm_gain, norm_bias, spatial_qkv, spatial_out, stale_codes, stale_exponents, temporal_qkv, temporal_out):
    head_count = C // HEAD
    scaling = HEAD ** (-0.5)
    time_embed = sinusoid(timestep.astype(jnp.float32), C).astype(jnp.bfloat16)
    time_shift = jnp.dot(time_embed, time_weight, preferred_element_type=jnp.float32)[0]
    latent_wide = latent.astype(jnp.float32)
    grouped = latent_wide.reshape(FRAMES, ROWS * W, GROUPS, C // GROUPS)
    group_mean = lax.optimization_barrier(jnp.mean(grouped, axis=(1, 3), keepdims=True))
    centered = grouped - group_mean
    group_var = lax.optimization_barrier(jnp.mean(centered * centered, axis=(1, 3), keepdims=True))
    normed = (centered * lax.rsqrt(group_var + 1e-05)).reshape(FRAMES, ROWS, W, C)
    normed_in = (normed * norm_gain + norm_bias + time_shift).astype(jnp.bfloat16)
    projected = jnp.dot(normed_in.reshape(-1, C), spatial_qkv, preferred_element_type=jnp.float32).reshape(FRAMES, ROWS, W, 3 * C)
    query_all = projected[..., :C].astype(jnp.bfloat16)
    fresh_kv = projected[..., C:].astype(jnp.bfloat16)
    factor = jnp.repeat(jnp.exp2(stale_exponents.astype(jnp.float32)), HEAD, axis=-1)[:, :, None, :]
    stale_in = (stale_codes.astype(jnp.float32) * factor).astype(jnp.bfloat16)
    residual_codes = ((normed_in.astype(jnp.float32) - stale_in.astype(jnp.float32)) / factor).astype(jnp.bfloat16)
    stale_kv = jnp.dot(stale_in.reshape(-1, C), spatial_qkv[:, C:], preferred_element_type=jnp.float32).astype(jnp.bfloat16).reshape(FRAMES, ROWS, W, 2 * C)
    band_count = ROWS // ROWS_DEV

    def band_attention(band_index):
        frame_index = band_index // band_count
        first_row = band_index % band_count * ROWS_DEV
        zero_index = jnp.zeros((), jnp.int32)
        band_query = lax.dynamic_slice(query_all, (frame_index, first_row, zero_index, zero_index), (1, ROWS_DEV, W, C))
        band_fresh = lax.dynamic_slice(fresh_kv, (frame_index, first_row, zero_index, zero_index), (1, ROWS_DEV, W, 2 * C))
        frame_kv = lax.dynamic_slice(stale_kv, (frame_index, zero_index, zero_index, zero_index), (1, ROWS, W, 2 * C))
        frame_kv = lax.dynamic_update_slice(frame_kv, band_fresh, (zero_index, first_row, zero_index, zero_index))
        query_heads = band_query.reshape(ROWS_DEV * W, head_count, HEAD).astype(jnp.float32)
        key_heads = frame_kv[..., :C].reshape(ROWS * W, head_count, HEAD).astype(jnp.float32)
        value_heads = frame_kv[..., C:].reshape(ROWS * W, head_count, HEAD).astype(jnp.float32)
        scores = jnp.einsum('qhd,khd->hqk', query_heads, key_heads) * scaling
        weights = jnp.exp(scores - lax.optimization_barrier(jnp.max(scores, axis=-1, keepdims=True)))
        denominator = lax.optimization_barrier(jnp.sum(weights, axis=-1))
        rounded = lax.optimization_barrier(weights.astype(jnp.bfloat16))
        numerator = jnp.einsum('hqk,khd->qhd', rounded.astype(jnp.float32), value_heads)
        return (numerator / jnp.transpose(denominator)[:, :, None]).astype(jnp.bfloat16).reshape(ROWS_DEV, W, C)
    attended = lax.map(band_attention, jnp.arange(FRAMES * band_count, dtype=jnp.int32)).reshape(FRAMES, ROWS, W, C)
    mixed_rows = jnp.dot(attended.reshape(-1, C), spatial_out, preferred_element_type=jnp.float32).reshape(FRAMES, ROWS, W, C)
    section_one = lax.optimization_barrier((latent_wide + mixed_rows).astype(jnp.bfloat16))
    frame_embed = sinusoid(jnp.arange(FRAMES, dtype=jnp.float32), C)
    shifted = section_one.astype(jnp.float32) + frame_embed[:, None, None, :]
    row_mean = lax.optimization_barrier(jnp.mean(shifted, axis=-1, keepdims=True))
    deviation = shifted - row_mean
    normed_t = (deviation * lax.rsqrt(lax.optimization_barrier(jnp.mean(deviation * deviation, axis=-1, keepdims=True)) + 1e-05)).astype(jnp.bfloat16)
    temporal_proj = jnp.dot(normed_t.reshape(-1, C), temporal_qkv, preferred_element_type=jnp.float32).astype(jnp.bfloat16)
    temporal_proj = temporal_proj.reshape(FRAMES, ROWS * W, 3, head_count, HEAD).astype(jnp.float32)
    temporal_scores = jnp.einsum('fphd,gphd->phfg', temporal_proj[:, :, 0], temporal_proj[:, :, 1]) * scaling
    temporal_weights = jnp.exp(temporal_scores - lax.optimization_barrier(jnp.max(temporal_scores, axis=-1, keepdims=True)))
    temporal_denominator = lax.optimization_barrier(jnp.sum(temporal_weights, axis=-1))
    temporal_rounded = lax.optimization_barrier(temporal_weights.astype(jnp.bfloat16))
    temporal_numerator = jnp.einsum('phfg,gphd->fphd', temporal_rounded.astype(jnp.float32), temporal_proj[:, :, 2])
    temporal_mix = (temporal_numerator / jnp.transpose(temporal_denominator, (2, 0, 1))[..., None]).astype(jnp.bfloat16)
    temporal_rows = jnp.dot(temporal_mix.reshape(-1, C), temporal_out, preferred_element_type=jnp.float32).reshape(FRAMES, ROWS, W, C)
    block_output = (section_one.astype(jnp.float32) + temporal_rows).astype(jnp.bfloat16)
    return (block_output, residual_codes)
```

```python
import functools
import math

import jax
import jax.numpy as jnp
import numpy as np
from jax import lax
from jax.experimental import pallas as pl
from jax.experimental.pallas import tpu as pltpu
from jax.sharding import PartitionSpec as P

HEAD = 64
HEADS = 5
C = 320
CP = 384
GROUP_WIDTH = 10
FRAMES = 16
ROWS = 64
W = 112
BAND = 224
MINE = 2 * BAND
BOTH = 2 * MINE
ZS = 8
PACK = 560
CHUNK = 32
WORKERS = 14
MESH = pl.DeviceIdType.MESH
F32 = jnp.float32
BF16 = jnp.bfloat16
LOG2E = 1.4426950408889634


def dot(a, b):
    return jnp.dot(a, b, preferred_element_type=F32)


def place():
    f, p = lax.axis_index("frame"), lax.axis_index("patch")
    return f // 4, f % 4, p // 4, (p // 2) % 2, p % 2


def device(x_lo, y, z, x_hi, core):
    return (x_lo * 4 + y, z * 4 + x_hi * 2 + core)


def remote(src, dst, send, recv, target):
    return pltpu.make_async_remote_copy(
        src_ref=src, dst_ref=dst, send_sem=send, recv_sem=recv, device_id=target, device_id_type=MESH
    )


def factor_row(ex_ref, frame, row, inverse):
    lane = lax.broadcasted_iota(jnp.int32, (1, C), 1) // HEAD
    power = jnp.zeros((1, C), jnp.int32)
    for block in range(C // HEAD):
        power = jnp.where(lane == block, ex_ref[frame, row, block], power)
    if inverse:
        power = -power
    out = jnp.full((1, C), 1.0, F32)
    for e in (-2, -1, 1, 2):
        out = jnp.where(power == e, 2.0**e, out)
    return out


def spatial_kernel(
    ts_ref, ex_ref, lat_ref, code_ref, tw_ref, gain_ref, bias_ref, wqkv_ref, wout_ref,
    sec_ref, res_ref,
    lat_in, stage, ring, st_mine, st_twin, st_comb, st_z, st_fin, st_own,
    w01, wlo, whi, wq, woutp, qcomp, qz, kt, vb, kt3, v3, m_ref, acc_ref, msend, mrecv,
    x_send, lat_recv, code_recv, rs_right, rs_left, rr_right, rr_left,
    tw_sems, z_send, z_recv, own_send, own_recv, q_sems, mg_sems,
):
    x_lo, y, z, x_hi, core = place()
    twin = device(x_lo, y, z, x_hi, 1 - core)
    right = device(x_lo, y, (z + 1) % ZS, x_hi, core)
    left = device(x_lo, y, (z + ZS - 1) % ZS, x_hi, core)
    sides = [device(1 - x_lo, y, z, parity, core) for parity in range(2)]
    zpeers = [device(x_lo, y, (z + d) % ZS, x_hi, core) for d in range(1, ZS)]

    barrier = pltpu.get_barrier_semaphore()
    for peer in [twin] + sides + zpeers:
        pl.semaphore_signal(barrier, inc=1, device_id=peer, device_id_type=MESH)
    pl.semaphore_wait(barrier, 3 + ZS - 1)

    def lat_copy(parity, band):
        return remote(lat_ref.at[parity], lat_in.at[band], x_send.at[parity], lat_recv.at[band], sides[parity])

    def code_copy(parity, band):
        return remote(stage.at[parity], ring.at[0, band], x_send.at[2 + parity], code_recv.at[band], sides[parity])

    for parity in range(2):
        lat_copy(parity, x_hi).start()
    for parity in range(2):
        rows = [
            code_ref[parity, r].astype(F32) * factor_row(ex_ref, parity, r, False) for r in range(2)
        ]
        for r in range(2):
            for slab in range(2):
                stage[parity, slab * BAND + r * W : slab * BAND + (r + 1) * W, :] = rows[r][
                    :, slab * 128 : (slab + 1) * 128
                ].astype(BF16)
        stage[parity, 2 * BAND :, :] = jnp.concatenate(
            [rows[0][:, 256:320], rows[1][:, 256:320]], axis=1
        ).astype(BF16)
        code_copy(parity, x_hi).start()

    def to_right(step, band):
        return remote(
            ring.at[step - 1, band], ring.at[step, band],
            rs_right.at[(step - 1) * 2 + band], rr_right.at[(step - 1) * 2 + band], right,
        )

    def to_left(step, band):
        return remote(
            ring.at[jnp.where(step == 1, 0, step + 2), band], ring.at[step + 3, band],
            rs_left.at[(step - 1) * 2 + band], rr_left.at[(step - 1) * 2 + band], left,
        )

    def far_right():
        return remote(ring.at[3, 0], ring.at[7, 0], rs_right.at[6], rr_right.at[6], right)

    def far_left():
        return remote(ring.at[6, 1], ring.at[7, 1], rs_left.at[6], rr_left.at[6], left)

    wq[...] = jnp.concatenate([wqkv_ref[:, :C], jnp.zeros((C, CP - C), BF16)], axis=1)
    pad = jnp.zeros((C, CP - C), BF16)
    wkv = jnp.concatenate([wqkv_ref[:, C : 2 * C], pad, wqkv_ref[:, 2 * C :], pad], axis=1)
    w01[...] = wkv[:256]
    wlo[:64] = wkv[256:]
    wlo[64:] = jnp.zeros((64, 2 * CP), BF16)
    whi[:64] = jnp.zeros((64, 2 * CP), BF16)
    whi[64:] = wkv[256:]
    woutp[:C] = wout_ref[...]
    woutp[C:] = jnp.zeros((CP - C, C), BF16)
    vb[:, CP:] = jnp.ones((BOTH, 128), BF16)
    for i in range(3):
        v3[i, :, CP:] = jnp.ones((MINE, 128), BF16)

    lane = lax.broadcasted_iota(jnp.int32, (1, C), 1)
    half = C // 2
    index = jnp.where(lane < half, lane, lane - half).astype(F32)
    angle = ts_ref[0].astype(F32) * jnp.exp(-math.log(10000.0) * index / half)
    embed = jnp.where(lane < half, jnp.cos(angle), jnp.sin(angle)).astype(BF16)
    shift = dot(jnp.broadcast_to(embed, (16, C)), tw_ref[...])[0:1]

    for band in range(2):
        code_copy(0, band).wait_recv()
        to_right(1, band).start()
        to_left(1, band).start()

    def two_rows(first, second):
        row = lax.broadcasted_iota(jnp.int32, (8, C), 0)
        return jnp.where(row == 0, first, jnp.where(row == 1, second, 0.0))

    for band in range(2):
        lat_copy(0, band).wait_recv()
    wide = lat_in[...].reshape(MINE, C).astype(F32)
    mean = jnp.sum(wide, axis=0, keepdims=True) / MINE
    deviation = wide - mean
    st_mine[...] = two_rows(mean, jnp.sum(deviation * deviation, axis=0, keepdims=True))
    to_twin = remote(st_mine, st_twin, tw_sems.at[0], tw_sems.at[1], twin)
    to_twin.start()
    to_twin.wait_recv()
    delta = st_mine[0:1] - st_twin[0:1]
    st_comb[...] = two_rows(
        (st_mine[0:1] + st_twin[0:1]) * 0.5, st_mine[1:2] + st_twin[1:2] + delta * delta * (MINE / 2)
    )
    z_copies = [remote(st_comb, st_z.at[d], z_send.at[d], z_recv.at[d], zpeers[d - 1]) for d in range(1, ZS)]
    for copy in z_copies:
        copy.start()

    def project(blocks):
        x01 = jnp.concatenate(
            [jnp.concatenate([ring[s, b, :BAND], ring[s, b, BAND : 2 * BAND]], axis=1) for s, b in blocks], axis=0
        )
        tail = jnp.concatenate([ring[s, b, 2 * BAND :] for s, b in blocks], axis=0)
        low, high = dot(tail, wlo[...]), dot(tail, whi[...])
        rest = []
        for i in range(len(blocks)):
            rest += [low[i * W : (i + 1) * W], high[i * W : (i + 1) * W]]
        both = (dot(x01, w01[...]) + jnp.concatenate(rest, axis=0)).astype(BF16)
        return both[:, :CP], both[:, CP:]

    stale_k, stale_v = project([(0, 0), (0, 1)])
    kt3[2] = stale_k.T
    v3[2, :, :CP] = stale_v

    for copy in z_copies:
        copy.wait_recv()
    means = [st_comb[0:1]] + [st_z[d, 0:1] for d in range(1, ZS)]
    total = sum(means[1:], means[0]) / ZS
    squares = st_comb[1:2]
    for d in range(1, ZS):
        squares = squares + st_z[d, 1:2]
    for one in means:
        squares = squares + (one - total) * (one - total) * (2 * MINE)
    g_row = lax.broadcasted_iota(jnp.int32, (C, C), 0) // GROUP_WIDTH
    g_col = lax.broadcasted_iota(jnp.int32, (C, C), 1) // GROUP_WIDTH
    same = (g_row == g_col).astype(F32)

    def group_sum(row):
        return jnp.dot(
            jnp.broadcast_to(row, (8, C)), same, preferred_element_type=F32, precision=lax.Precision.HIGHEST
        )[0:1]

    cells = ROWS * W
    group_mean = group_sum(total) / GROUP_WIDTH
    off = total - group_mean
    group_var = group_sum(squares + off * off * cells) / (cells * GROUP_WIDTH)
    rstd = lax.rsqrt(group_var + 1e-05)
    st_fin[...] = two_rows(group_mean, rstd)
    own_copies = [
        remote(st_fin, st_own.at[x_hi], own_send.at[i], own_recv.at[x_hi], sides[i]) for i in range(2)
    ]
    for copy in own_copies:
        copy.start()

    gain, bias = gain_ref[...], bias_ref[...]
    normed = ((wide - group_mean) * rstd * gain + bias + shift).astype(BF16)
    qcomp[0] = (dot(normed, wq[...]) * (HEAD**-0.5 * LOG2E)).astype(BF16)
    q_copy = remote(qcomp.at[0], qcomp.at[1], q_sems.at[0], q_sems.at[1], twin)
    q_copy.start()
    fresh = (dot(normed[:, :256], w01[...]) + dot(normed[:, 256:], wlo[:64])).astype(BF16)
    fresh_k, fresh_v = fresh[:, :CP], fresh[:, CP:]
    kt3[0] = jnp.concatenate([fresh_k[:BAND], stale_k[BAND:]], axis=0).T
    kt3[1] = jnp.concatenate([stale_k[:BAND], fresh_k[BAND:]], axis=0).T
    v3[0, :BAND, :CP] = fresh_v[:BAND]
    v3[0, BAND:, :CP] = stale_v[BAND:]
    v3[1, :BAND, :CP] = stale_v[:BAND]
    v3[1, BAND:, :CP] = fresh_v[BAND:]

    m_ref[...] = jnp.full(m_ref.shape, -1e30, F32)
    acc_ref[...] = jnp.zeros(acc_ref.shape, F32)
    lane128 = lax.broadcasted_iota(jnp.int32, (1, 128), 1)
    low_half = lane128 < HEAD

    def pass_on(step):
        for band in range(2):
            to_right(step, band).wait_recv()
            to_right(step + 1, band).start()
            to_left(step, band).wait_recv()
            to_left(step + 1, band).start()

    pass_on(1)
    q_copy.wait_recv()
    for who in range(2):
        for h in range(HEADS):
            slab = qcomp[who, :, (h // 2) * 128 : (h // 2) * 128 + 128]
            keep = low_half if h % 2 == 0 else jnp.logical_not(low_half)
            qz[h, who * MINE : (who + 1) * MINE, :] = jnp.where(keep, slab, jnp.zeros_like(slab))

    def attend(scores_of, values_of):
        scores = scores_of(0)
        for h in range(HEADS):
            following = scores_of(h + 1) if h < HEADS - 1 else None
            old = m_ref[h][:, :1]
            peak = jnp.maximum(old, jnp.max(scores, axis=1, keepdims=True))
            weights = jnp.exp2(scores - peak).astype(BF16)
            m_ref[h] = jnp.broadcast_to(peak, (BOTH, 128))
            acc_ref[h] = acc_ref[h] * jnp.exp2(old - peak) + values_of(h, weights)
            scores = following

    parts = ((0, 0, BAND), (1, BAND, MINE), (2, MINE, BOTH))

    def own_scores(h):
        s = h // 2 * 128
        return jnp.concatenate([dot(qz[h, a:b], kt3[i, s : s + 128]) for i, a, b in parts], axis=0)

    def own_values(h, weights):
        s = h // 2 * 128
        return jnp.concatenate(
            [
                dot(weights[a:b], jnp.concatenate([v3[i, :, s : s + 128], v3[i, :, CP:]], axis=1))
                for i, a, b in parts
            ],
            axis=0,
        )

    attend(own_scores, own_values)

    def block(blocks):
        keys = len(blocks) * BAND
        k, v = project(blocks)
        kt[:, :keys] = k.T
        vb[:keys, :CP] = v

        def scores_of(h):
            s = h // 2 * 128
            return dot(qz[h], kt[s : s + 128, :keys])

        def values_of(h, weights):
            s = h // 2 * 128
            return dot(weights, jnp.concatenate([vb[:keys, s : s + 128], vb[:keys, CP:]], axis=1))

        attend(scores_of, values_of)

    def ring_turn(i, carry):
        @pl.when(i == 1)
        def _():
            pass_on(2)

        @pl.when(i == 2)
        def _():
            for band in range(2):
                to_right(3, band).wait_recv()
                to_left(3, band).wait_recv()
            far_right().start()
            far_left().start()

        block([(i, 0), (i, 1), (i + 3, 0), (i + 3, 1)])
        return carry

    lax.fori_loop(1, 4, ring_turn, 0)
    far_right().wait_recv()
    far_left().wait_recv()
    block([(7, 0), (7, 1)])

    stats = jnp.zeros((MINE, 128), F32)
    for h in range(HEADS):
        stats = jnp.where(lane128 == h, m_ref[h, MINE:], stats)
        stats = jnp.where(lane128 == 8 + h, acc_ref[h, MINE:, 128:], stats)
    for slab in range(3):
        one = acc_ref[2 * slab, MINE:, :128]
        if slab < 2:
            one = jnp.where(low_half, one, acc_ref[2 * slab + 1, MINE:, :128])
        msend[:, slab * 128 : (slab + 1) * 128] = one
    msend[:, CP:] = stats
    merge = remote(msend, mrecv, mg_sems.at[0], mg_sems.at[1], twin)
    merge.start()

    for parity in range(2):
        remote(st_fin, st_own.at[parity], own_send.at[0], own_recv.at[parity], sides[0]).wait_recv()
        for r in range(2):
            own = lat_ref[parity, r].astype(F32)
            normed_own = ((own - st_own[parity, 0:1]) * st_own[parity, 1:2] * gain + bias + shift).astype(BF16)
            stale_own = code_ref[parity, r].astype(F32) * factor_row(ex_ref, parity, r, False)
            res_ref[parity, r] = (
                (normed_own.astype(F32) - stale_own) * factor_row(ex_ref, parity, r, True)
            ).astype(BF16)

    merge.wait_recv()
    keep_own, keep_other, sums = [], [], []
    for h in range(HEADS):
        mine, other = m_ref[h, :MINE], mrecv[:, CP + h : CP + h + 1]
        peak = jnp.maximum(mine, other)
        a, b = jnp.exp2(mine - peak), jnp.exp2(other - peak)
        keep_own.append(a)
        keep_other.append(b)
        sums.append(acc_ref[h, :MINE, 128:] * a + mrecv[:, CP + 8 + h : CP + 9 + h] * b)
    slabs = []
    for slab in range(3):
        e, o = 2 * slab, min(2 * slab + 1, HEADS - 1)

        def pick(values):
            return values[e] if e == o else jnp.where(low_half, values[e], values[o])

        own_sum = pick([acc_ref[h, :MINE, :128] for h in range(HEADS)])
        joined = own_sum * pick(keep_own) + mrecv[:, slab * 128 : (slab + 1) * 128] * pick(keep_other)
        slabs.append((joined / pick(sums)).astype(BF16))
    attended = jnp.concatenate(slabs, axis=1)
    sec_ref[...] = (wide_again(lat_in) + dot(attended, woutp[...])).astype(BF16)

    for parity in range(2):
        lat_copy(parity, x_hi).wait_send()
        code_copy(parity, x_hi).wait_send()
    to_twin.wait_send()
    for copy in z_copies + own_copies:
        copy.wait_send()
    q_copy.wait_send()
    merge.wait_send()
    for step in range(1, 4):
        for band in range(2):
            to_right(step, band).wait_send()
            to_left(step, band).wait_send()
    far_right().wait_send()
    far_left().wait_send()


def wide_again(lat_in):
    return lat_in[...].reshape(MINE, C).astype(F32)


def worker_place(j):
    owner = j // 2
    return 1 - owner // 4, owner % 4, j % 2


def temporal_kernel(
    sec_ref, embed_ref, wqkv_ref, wout_ref, out_ref,
    xin, yout, wp, woutp, f_send, f_recv, b_send, b_recv, local_sem,
):
    x_lo, y, z, x_hi, core = place()
    frame = 2 * ((1 - x_lo) * 4 + y) + x_hi

    barrier = pltpu.get_barrier_semaphore()
    places = [worker_place(j) for j in range(FRAMES)]
    devices = [device(a, b, z, c, core) for a, b, c in places]
    for j in range(FRAMES):

        @pl.when(frame != j)
        def _():
            pl.semaphore_signal(barrier, inc=1, device_id=devices[j], device_id_type=MESH)

    pl.semaphore_wait(barrier, FRAMES - 1)

    def forward(j, source):
        return remote(
            sec_ref.at[pl.ds(j * CHUNK, CHUNK)], xin.at[source], f_send.at[j], f_recv.at[source], devices[j]
        )

    for j in range(WORKERS):

        @pl.when(frame != j)
        def _():
            forward(j, frame).start()

        @pl.when(frame == j)
        def _():
            pltpu.make_async_copy(sec_ref.at[pl.ds(j * CHUNK, CHUNK)], xin.at[j], local_sem.at[0]).start()

    pad = jnp.zeros((C, CP - C), BF16)
    wp[...] = jnp.concatenate(
        [wqkv_ref[:, :C], pad, wqkv_ref[:, C : 2 * C], pad, wqkv_ref[:, 2 * C :], pad], axis=1
    )
    woutp[:C] = wout_ref[...]
    woutp[C:] = jnp.zeros((CP - C, C), BF16)

    band = frame // 7
    spot = frame % 7

    def back(target):
        return remote(
            yout.at[pl.ds(2 * target, 2)],
            out_ref.at[pl.ds(0, 2), pl.ds(spot * CHUNK, CHUNK)],
            b_send.at[target],
            b_recv.at[spot],
            device(target // 4, target % 4, z, band, core),
        )

    def back_local(target):
        return pltpu.make_async_copy(
            yout.at[pl.ds(2 * target, 2)],
            out_ref.at[pl.ds(0, 2), pl.ds(spot * CHUNK, CHUNK)],
            local_sem.at[1],
        )

    here = x_lo * 4 + y

    @pl.when(frame < WORKERS)
    def _():
        for j in range(FRAMES):

            @pl.when(frame != j)
            def _():
                forward(0, j).wait_recv()

            @pl.when(frame == j)
            def _():
                pltpu.make_async_copy(sec_ref.at[pl.ds(0, CHUNK)], xin.at[j], local_sem.at[0]).wait()

        low_half = lax.broadcasted_iota(jnp.int32, (1, 128), 1) < HEAD
        tile = FRAMES * 16
        row_cell = lax.broadcasted_iota(jnp.int32, (tile, tile), 0) % 16
        col_cell = lax.broadcasted_iota(jnp.int32, (tile, tile), 1) % 16
        same = row_cell == col_cell
        for part in range(CHUNK // 16):
            section = xin[:, part * 16 : (part + 1) * 16, :].astype(F32)
            shifted = (section + embed_ref[...][:, None, :]).reshape(tile, C)
            mean = jnp.mean(shifted, axis=-1, keepdims=True)
            deviation = shifted - mean
            normed = (
                deviation * lax.rsqrt(jnp.mean(deviation * deviation, axis=-1, keepdims=True) + 1e-05)
            ).astype(BF16)
            proj = dot(normed, wp[...]).astype(BF16)
            mixed = []
            for slab in range(3):
                q = proj[:, slab * 128 : (slab + 1) * 128]
                k = proj[:, CP + slab * 128 : CP + (slab + 1) * 128]
                v = proj[:, 2 * CP + slab * 128 : 2 * CP + (slab + 1) * 128]
                halves = []
                for h in range(2 if slab < 2 else 1):
                    keep = low_half if h == 0 else jnp.logical_not(low_half)
                    scores = lax.dot_general(
                        jnp.where(keep, q, jnp.zeros_like(q)), k, (((1,), (1,)), ((), ())),
                        preferred_element_type=F32,
                    ) * (HEAD**-0.5)
                    scores = jnp.where(same, scores, -1e30)
                    weights = jnp.exp(scores - jnp.max(scores, axis=1, keepdims=True))
                    below = jnp.sum(weights, axis=1, keepdims=True)
                    halves.append(dot(weights.astype(BF16), v) / below)
                mixed.append(halves[0] if slab == 2 else jnp.where(low_half, halves[0], halves[1]))
            mix = jnp.concatenate(mixed, axis=1).astype(BF16)
            result = section.reshape(tile, C) + dot(mix, woutp[...])
            yout[:, part * 16 : (part + 1) * 16, :] = result.astype(BF16).reshape(FRAMES, 16, C)
        for target in range(8):
            stays = jnp.logical_and(here == target, x_hi == band)

            @pl.when(stays)
            def _():
                back_local(target).start()

            @pl.when(jnp.logical_not(stays))
            def _():
                back(target).start()

    for s in range(7):
        source = x_hi * 7 + s

        @pl.when(frame == source)
        def _():
            pltpu.make_async_copy(
                yout.at[pl.ds(0, 2)], out_ref.at[pl.ds(0, 2), pl.ds(s * CHUNK, CHUNK)], local_sem.at[1]
            ).wait()

        @pl.when(frame != source)
        def _():
            remote(
                yout.at[pl.ds(0, 2)], out_ref.at[pl.ds(0, 2), pl.ds(s * CHUNK, CHUNK)],
                b_send.at[0], b_recv.at[s], devices[0],
            ).wait_recv()

    for j in range(WORKERS):

        @pl.when(frame != j)
        def _():
            forward(j, frame).wait_send()

    @pl.when(frame < WORKERS)
    def _():
        for target in range(8):

            @pl.when(jnp.logical_not(jnp.logical_and(here == target, x_hi == band)))
            def _():
                back(target).wait_send()


def frame_table():
    half = C // 2
    frequency = np.exp(-math.log(10000.0) * np.arange(half) / half)
    angles = np.arange(FRAMES)[:, None] * frequency
    return np.concatenate([np.cos(angles), np.sin(angles)], axis=-1).astype(np.float32)


VM = pl.BlockSpec(memory_space=pltpu.VMEM)
SM = pl.BlockSpec(memory_space=pltpu.SMEM)


def body(
    latent, timestep, time_weight, norm_gain, norm_bias, spatial_qkv, spatial_out,
    stale_codes, stale_exponents, temporal_qkv, temporal_out,
):
    dma = pltpu.SemaphoreType.DMA
    section, residual = pl.pallas_call(
        spatial_kernel,
        out_shape=(
            jax.ShapeDtypeStruct((MINE, C), BF16),
            jax.ShapeDtypeStruct((2, 2, W, C), BF16),
        ),
        in_specs=[SM, SM] + [VM] * 7,
        out_specs=(VM, VM),
        scratch_shapes=[
            pltpu.VMEM((2, 2, W, C), BF16),
            pltpu.VMEM((2, PACK, 128), BF16),
            pltpu.VMEM((ZS, 2, PACK, 128), BF16),
            pltpu.VMEM((8, C), F32),
            pltpu.VMEM((8, C), F32),
            pltpu.VMEM((8, C), F32),
            pltpu.VMEM((ZS, 8, C), F32),
            pltpu.VMEM((8, C), F32),
            pltpu.VMEM((2, 8, C), F32),
            pltpu.VMEM((256, 2 * CP), BF16),
            pltpu.VMEM((128, 2 * CP), BF16),
            pltpu.VMEM((128, 2 * CP), BF16),
            pltpu.VMEM((C, CP), BF16),
            pltpu.VMEM((CP, C), BF16),
            pltpu.VMEM((2, MINE, CP), BF16),
            pltpu.VMEM((HEADS, BOTH, 128), BF16),
            pltpu.VMEM((CP, BOTH), BF16),
            pltpu.VMEM((BOTH, 512), BF16),
            pltpu.VMEM((3, CP, MINE), BF16),
            pltpu.VMEM((3, MINE, 512), BF16),
            pltpu.VMEM((HEADS, BOTH, 128), F32),
            pltpu.VMEM((HEADS, BOTH, 256), F32),
            pltpu.VMEM((MINE, 512), F32),
            pltpu.VMEM((MINE, 512), F32),
            dma((4,)), dma((2,)), dma((2,)), dma((7,)), dma((7,)), dma((7,)), dma((7,)),
            dma((2,)), dma((ZS,)), dma((ZS,)), dma((2,)), dma((2,)), dma((2,)), dma((2,)),
        ],
        compiler_params=pltpu.CompilerParams(
            collective_id=0, has_side_effects=True, vmem_limit_bytes=60 * 2**20
        ),
        name="spatial",
    )(
        timestep, stale_exponents, latent, stale_codes, time_weight,
        norm_gain.reshape(1, C), norm_bias.reshape(1, C), spatial_qkv, spatial_out,
    )
    output = pl.pallas_call(
        temporal_kernel,
        out_shape=jax.ShapeDtypeStruct((2, BAND, C), BF16),
        in_specs=[VM] * 4,
        out_specs=VM,
        scratch_shapes=[
            pltpu.VMEM((FRAMES, CHUNK, C), BF16),
            pltpu.VMEM((FRAMES, CHUNK, C), BF16),
            pltpu.VMEM((C, 3 * CP), BF16),
            pltpu.VMEM((CP, C), BF16),
            dma((WORKERS,)), dma((FRAMES,)), dma((8,)), dma((7,)), dma((2,)),
        ],
        compiler_params=pltpu.CompilerParams(
            collective_id=1, has_side_effects=True, vmem_limit_bytes=40 * 2**20
        ),
        name="temporal",
    )(section, jnp.asarray(frame_table()), temporal_qkv, temporal_out)
    return output.reshape(2, 2, W, C), residual


def solution(mesh):
    placed = (
        P("frame", "patch", None, None),
        P(),
        P(),
        P(),
        P(),
        P(),
        P(),
        P("frame", "patch", None, None),
        P("frame", "patch", None),
        P(),
        P(),
    )
    return jax.shard_map(
        body,
        mesh=mesh,
        in_specs=placed,
        out_specs=(P("frame", "patch", None, None), P("frame", "patch", None, None)),
        check_vma=False,
    )
```

```python
import functools
import math

import jax
import jax.numpy as jnp
import numpy as np
from jax import lax
from jax.experimental import pallas as pl
from jax.experimental.pallas import tpu as pltpu
from jax.sharding import PartitionSpec as P

HEAD = 64
HEADS = 5
C = 320
CP = 384
GROUP_WIDTH = 10
FRAMES = 16
ROWS = 64
W = 112
BAND = 224
MINE = 2 * BAND
BOTH = 2 * MINE
ZS = 8
PACK = 560
CELLS = 32
WORKERS = 14
KEYS = 8 * BAND
FIRST = 512
MESH = pl.DeviceIdType.MESH
F32 = jnp.float32
BF16 = jnp.bfloat16
LOG2E = 1.4426950408889634


def dot(a, b):
    return jnp.dot(a, b, preferred_element_type=F32)


def place():
    f, p = lax.axis_index("frame"), lax.axis_index("patch")
    return f // 4, f % 4, p // 4, (p // 2) % 2, p % 2


def device(x_lo, y, z, x_hi, core):
    return (x_lo * 4 + y, z * 4 + x_hi * 2 + core)


def remote(src, dst, send, recv, target):
    return pltpu.make_async_remote_copy(
        src_ref=src, dst_ref=dst, send_sem=send, recv_sem=recv, device_id=target, device_id_type=MESH
    )


def factor_row(ex_ref, frame, row):
    lane = lax.broadcasted_iota(jnp.int32, (1, C), 1) // HEAD
    power = jnp.zeros((1, C), jnp.int32)
    for block in range(C // HEAD):
        power = jnp.where(lane == block, ex_ref[frame, row, block], power)
    out = jnp.full((1, C), 1.0, F32)
    for e in (-1, 1, 2):
        out = jnp.where(power == e, 2.0**e, out)
    return out


def rows_of(*parts):
    row = lax.broadcasted_iota(jnp.int32, (8, C), 0)
    out = jnp.zeros((8, C), F32)
    for i, part in enumerate(parts):
        out = jnp.where(row == i, part, out)
    return out


def worker_device(j, z, core):
    owner = j // 2
    return device(1 - owner // 4, owner % 4, z, j % 2, core)


def kernel(
    ts_ref, ex_ref, lat_ref, code_ref, tw_ref, gain_ref, bias_ref, wqkv_ref, wout_ref, embed_ref,
    wt_ref, wtout_ref,
    out_ref, res_ref,
    lat_in, wide_ref, stage, ring, st_mine, st_twin, st_comb, st_z, st_side, st_x, st_fin, st_own,
    w01, wlo, whi, wq, woutp, wp, wtoutp, qcomp, qz, kb, kt, vb, kt3, v3, m_ref, acc_ref, msend, mrecv,
    sec, xin, yout, got,
    x_send, lat_recv, code_recv, rs_right, rs_left, rr_right, rr_left,
    tw_sems, z_send, z_recv, sx_send, sx_recv, own_send, own_recv, q_sems, mg_sems,
    f_send, f_recv, b_send, b_recv, local_sem,
):
    x_lo, y, z, x_hi, core = place()
    frame = 2 * ((1 - x_lo) * 4 + y) + x_hi
    twin = device(x_lo, y, z, x_hi, 1 - core)
    right = device(x_lo, y, (z + 1) % ZS, x_hi, core)
    left = device(x_lo, y, (z + ZS - 1) % ZS, x_hi, core)
    sides = [device(1 - x_lo, y, z, parity, core) for parity in range(2)]
    zpeers = [device(x_lo, y, (z + d) % ZS, x_hi, core) for d in range(1, ZS)]

    barrier = pltpu.get_barrier_semaphore()
    plane = [worker_device((frame + k) % FRAMES, z, core) for k in range(1, FRAMES)]
    for peer in [twin] + zpeers + plane:
        pl.semaphore_signal(barrier, inc=1, device_id=peer, device_id_type=MESH)
    pl.semaphore_wait(barrier, 1 + ZS - 1 + FRAMES - 1)

    def lat_copy(parity, band):
        return remote(lat_ref.at[parity], lat_in.at[band], x_send.at[parity], lat_recv.at[band], sides[parity])

    def code_copy(parity, band):
        return remote(stage.at[parity], ring.at[0, band], x_send.at[2 + parity], code_recv.at[band], sides[parity])

    for parity in range(2):
        rows = [
            code_ref[parity, r].astype(F32).T * factor_row(ex_ref, parity, r) for r in range(2)
        ]
        for r in range(2):
            for slab in range(2):
                stage[parity, slab * BAND + r * W : slab * BAND + (r + 1) * W, :] = rows[r][
                    :, slab * 128 : (slab + 1) * 128
                ].astype(BF16)
        stage[parity, 2 * BAND :, :] = jnp.concatenate(
            [rows[0][:, 256:320], rows[1][:, 256:320]], axis=1
        ).astype(BF16)
        code_copy(parity, x_hi).start()
    for parity in range(2):
        lat_copy(parity, x_hi).start()

    stats = []
    for parity in range(2):
        own = jnp.concatenate([lat_ref[parity, r].astype(F32).T for r in range(2)], axis=0)
        mean = jnp.sum(own, axis=0, keepdims=True) / BAND
        deviation = own - mean
        stats += [mean, jnp.sum(deviation * deviation, axis=0, keepdims=True)]
    st_mine[...] = rows_of(*stats)
    to_twin = remote(st_mine, st_twin, tw_sems.at[0], tw_sems.at[1], twin)
    to_twin.start()

    def to_right(step, band):
        return remote(
            ring.at[step - 1, band], ring.at[step, band],
            rs_right.at[(step - 1) * 2 + band], rr_right.at[(step - 1) * 2 + band], right,
        )

    def to_left(step, band):
        return remote(
            ring.at[0 if step == 1 else step + 2, band], ring.at[step + 3, band],
            rs_left.at[(step - 1) * 2 + band], rr_left.at[(step - 1) * 2 + band], left,
        )

    def far_right():
        return remote(ring.at[3, 0], ring.at[7, 0], rs_right.at[6], rr_right.at[6], right)

    def far_left():
        return remote(ring.at[6, 1], ring.at[7, 1], rs_left.at[6], rr_left.at[6], left)

    pad = jnp.zeros((C, CP - C), BF16)
    wq[...] = jnp.concatenate([wqkv_ref[:, :C], pad], axis=1)
    wkv = jnp.concatenate([wqkv_ref[:, C : 2 * C], pad, wqkv_ref[:, 2 * C :], pad], axis=1)
    w01[...] = wkv[:256]
    wlo[:64] = wkv[256:]
    wlo[64:] = jnp.zeros((64, 2 * CP), BF16)
    whi[:64] = jnp.zeros((64, 2 * CP), BF16)
    whi[64:] = wkv[256:]

    to_twin.wait_recv()
    combined = []
    for parity in range(2):
        i = 2 * parity
        delta = st_mine[i : i + 1] - st_twin[i : i + 1]
        combined += [
            (st_mine[i : i + 1] + st_twin[i : i + 1]) * 0.5,
            st_mine[i + 1 : i + 2] + st_twin[i + 1 : i + 2] + delta * delta * (BAND / 2),
        ]
    st_comb[...] = rows_of(*combined)
    z_copies = [remote(st_comb, st_z.at[d], z_send.at[d], z_recv.at[d], zpeers[d - 1]) for d in range(1, ZS)]
    for copy in z_copies:
        copy.start()

    woutp[:C] = wout_ref[...]
    woutp[C:] = jnp.zeros((CP - C, C), BF16)
    wp[...] = jnp.concatenate([wt_ref[:, :C], pad, wt_ref[:, C : 2 * C], pad, wt_ref[:, 2 * C :], pad], axis=1)
    wtoutp[:C] = wtout_ref[...]
    wtoutp[C:] = jnp.zeros((CP - C, C), BF16)
    vb[:, CP:] = jnp.ones((KEYS, 128), BF16)
    for i in range(3):
        v3[i, :, CP:] = jnp.ones((FIRST, 128), BF16)

    lane = lax.broadcasted_iota(jnp.int32, (1, C), 1)
    half = C // 2
    index = jnp.where(lane < half, lane, lane - half).astype(F32)
    angle = ts_ref[0].astype(F32) * jnp.exp(-math.log(10000.0) * index / half)
    embed = jnp.where(lane < half, jnp.cos(angle), jnp.sin(angle)).astype(BF16)
    shift = dot(jnp.broadcast_to(embed, (16, C)), tw_ref[...])[0:1]
    gain = gain_ref[...].reshape(1, C)
    bias = bias_ref[...].reshape(1, C)

    for copy in z_copies:
        copy.wait_recv()
    side_copies = []
    for parity in range(2):
        i = 2 * parity
        means = [st_comb[i : i + 1]] + [st_z[d, i : i + 1] for d in range(1, ZS)]
        total = sum(means[1:], means[0]) / ZS
        squares = st_comb[i + 1 : i + 2]
        for d in range(1, ZS):
            squares = squares + st_z[d, i + 1 : i + 2]
        for one in means:
            squares = squares + (one - total) * (one - total) * (2 * BAND)
        st_side[parity] = rows_of(total, squares)
        copy = remote(st_side.at[parity], st_x.at[x_hi], sx_send.at[parity], sx_recv.at[x_hi], sides[parity])
        copy.start()
        side_copies.append(copy)

    code_copy(0, 0).wait_recv()
    to_right(1, 0).start()
    code_copy(0, 1).wait_recv()
    to_left(1, 1).start()
    to_right(1, 1).start()
    to_left(1, 0).start()

    def project(blocks):
        x01 = jnp.concatenate(
            [jnp.concatenate([ring[s, b, :BAND], ring[s, b, BAND : 2 * BAND]], axis=1) for s, b in blocks], axis=0
        )
        tail = jnp.concatenate([ring[s, b, 2 * BAND :] for s, b in blocks], axis=0)
        low, high = dot(tail, wlo[...]), dot(tail, whi[...])
        rest = []
        for i in range(len(blocks)):
            rest += [low[i * W : (i + 1) * W], high[i * W : (i + 1) * W]]
        both = (dot(x01, w01[...]) + jnp.concatenate(rest, axis=0)).astype(BF16)
        return both[:, :CP], both[:, CP:]

    stale_k, stale_v = project([(0, 0), (0, 1)])

    for band in range(2):
        remote(
            st_side.at[0], st_x.at[band], sx_send.at[0], sx_recv.at[band], sides[0]
        ).wait_recv()
    total = (st_x[0, 0:1] + st_x[1, 0:1]) * 0.5
    delta = st_x[0, 0:1] - st_x[1, 0:1]
    cells = ROWS * W
    squares = st_x[0, 1:2] + st_x[1, 1:2] + delta * delta * (cells / 4)
    g_row = lax.broadcasted_iota(jnp.int32, (C, C), 0) // GROUP_WIDTH
    g_col = lax.broadcasted_iota(jnp.int32, (C, C), 1) // GROUP_WIDTH
    same_group = (g_row == g_col).astype(F32)

    def group_sum(row):
        return jnp.dot(
            jnp.broadcast_to(row, (8, C)), same_group, preferred_element_type=F32, precision=lax.Precision.HIGHEST
        )[0:1]

    group_mean = group_sum(total) / GROUP_WIDTH
    off = total - group_mean
    group_var = group_sum(squares + off * off * cells) / (cells * GROUP_WIDTH)
    rstd = lax.rsqrt(group_var + 1e-05)
    st_fin[...] = rows_of(group_mean, rstd)
    own_copies = [
        remote(st_fin, st_own.at[x_hi], own_send.at[i], own_recv.at[x_hi], sides[i]) for i in range(2)
    ]
    for copy in own_copies:
        copy.start()

    for band in range(2):
        lat_copy(0, band).wait_recv()
        for r in range(2):
            wide_ref[band * BAND + r * W : band * BAND + (r + 1) * W] = (
                lat_in[band, r].astype(F32).T.astype(BF16)
            )
    wide = wide_ref[...].astype(F32)
    normed = ((wide - group_mean) * rstd * gain + bias + shift).astype(BF16)
    qcomp[0] = (dot(normed, wq[...]) * (HEAD**-0.5 * LOG2E)).astype(BF16)
    q_copy = remote(qcomp.at[0], qcomp.at[1], q_sems.at[0], q_sems.at[1], twin)
    q_copy.start()
    fresh = (dot(normed[:, :256], w01[...]) + dot(normed[:, 256:], wlo[:64])).astype(BF16)
    fresh_k, fresh_v = fresh[:, :CP], fresh[:, CP:]

    def pass_right(step, band):
        to_right(step, band).wait_recv()
        to_right(step + 1, band).start()

    def pass_left(step, band):
        to_left(step, band).wait_recv()
        to_left(step + 1, band).start()

    pass_right(1, 0)
    pass_left(1, 1)
    pass_right(1, 1)
    pass_left(1, 0)
    first_k, first_v = project([(1, 0), (1, 1), (4, 0), (4, 1)])
    pass_right(2, 0)
    pass_left(2, 1)
    second_k, second_v = project([(2, 0), (5, 1)])
    lead = FIRST - MINE
    own_k = [
        jnp.concatenate([fresh_k[:BAND], stale_k[BAND:], first_k[:lead]], axis=0),
        jnp.concatenate([stale_k[:BAND], fresh_k[BAND:], first_k[:lead]], axis=0),
        jnp.concatenate([stale_k, first_k[:lead]], axis=0),
    ]
    own_v = [
        jnp.concatenate([fresh_v[:BAND], stale_v[BAND:], first_v[:lead]], axis=0),
        jnp.concatenate([stale_v[:BAND], fresh_v[BAND:], first_v[:lead]], axis=0),
        jnp.concatenate([stale_v, first_v[:lead]], axis=0),
    ]
    for i in range(3):
        kt3[i] = own_k[i].T
        v3[i, :, :CP] = own_v[i]
    rest = KEYS - FIRST
    kt[:, :rest] = jnp.concatenate([first_k[lead:], second_k], axis=0).T
    vb[: 2 * MINE - lead, :CP] = first_v[lead:]
    vb[2 * MINE - lead : rest, :CP] = second_v

    lane128 = lax.broadcasted_iota(jnp.int32, (1, 128), 1)
    low_half = lane128 < HEAD
    q_copy.wait_recv()
    for who in range(2):
        for h in range(HEADS):
            slab = qcomp[who, :, (h // 2) * 128 : (h // 2) * 128 + 128]
            keep = low_half if h % 2 == 0 else jnp.logical_not(low_half)
            qz[h, who * MINE : (who + 1) * MINE, :] = jnp.where(keep, slab, jnp.zeros_like(slab))

    def attend(scores_of, values_of, first, between):
        scores = scores_of(0)
        for h in range(HEADS):
            following = scores_of(h + 1) if h < HEADS - 1 else None
            peak = jnp.max(scores, axis=1, keepdims=True)
            if not first:
                old = m_ref[h][:, :1]
                peak = jnp.maximum(old, peak)
            weights = jnp.exp2(scores - peak).astype(BF16)
            m_ref[h] = jnp.broadcast_to(peak, (BOTH, 128))
            if first:
                acc_ref[h] = values_of(h, weights)
            else:
                acc_ref[h] = acc_ref[h] * jnp.exp2(old - peak) + values_of(h, weights)
            scores = following
            if h in between:
                between[h]()

    parts = ((0, 0, BAND), (1, BAND, MINE), (2, MINE, BOTH))

    def own_scores(h):
        s = h // 2 * 128
        own = jnp.concatenate([dot(qz[h, a:b], kt3[i, s : s + 128]) for i, a, b in parts], axis=0)
        return jnp.concatenate([own, dot(qz[h], kt[s : s + 128, :rest])], axis=1)

    def own_values(h, weights):
        s = h // 2 * 128
        own = jnp.concatenate(
            [
                dot(weights[a:b, :FIRST], jnp.concatenate([v3[i, :, s : s + 128], v3[i, :, CP:]], axis=1))
                for i, a, b in parts
            ],
            axis=0,
        )
        return own + dot(weights[:, FIRST:], jnp.concatenate([vb[:rest, s : s + 128], vb[:rest, CP:]], axis=1))

    def middle():
        pass_right(2, 1)
        pass_left(2, 0)

    def late():
        to_right(3, 0).wait_recv()
        far_right().start()
        to_left(3, 1).wait_recv()
        far_left().start()

    attend(own_scores, own_values, True, {1: middle, 3: late})

    to_right(3, 1).wait_recv()
    to_left(3, 0).wait_recv()
    k, v = project([(2, 1), (5, 0), (3, 0), (3, 1), (6, 0), (6, 1)])
    kb[: 6 * BAND] = k
    vb[: 6 * BAND, :CP] = v
    far_right().wait_recv()
    far_left().wait_recv()
    k, v = project([(7, 0), (7, 1)])
    kb[6 * BAND :] = k
    vb[6 * BAND :, :CP] = v
    kt[...] = kb[...].T

    def scores_of(h):
        s = h // 2 * 128
        return dot(qz[h], kt[s : s + 128])

    def values_of(h, weights):
        s = h // 2 * 128
        return dot(weights, jnp.concatenate([vb[:, s : s + 128], vb[:, CP:]], axis=1))

    attend(scores_of, values_of, False, {})

    notes = jnp.zeros((MINE, 128), F32)
    for h in range(HEADS):
        notes = jnp.where(lane128 == h, m_ref[h, MINE:], notes)
        notes = jnp.where(lane128 == 8 + h, acc_ref[h, MINE:, 128:], notes)
    for slab in range(3):
        one = acc_ref[2 * slab, MINE:, :128]
        if slab < 2:
            one = jnp.where(low_half, one, acc_ref[2 * slab + 1, MINE:, :128])
        msend[:, slab * 128 : (slab + 1) * 128] = one
    msend[:, CP:] = notes
    merge = remote(msend, mrecv, mg_sems.at[0], mg_sems.at[1], twin)
    merge.start()

    for parity in range(2):
        remote(st_fin, st_own.at[parity], own_send.at[0], own_recv.at[parity], sides[0]).wait_recv()
        factors = [factor_row(ex_ref, parity, r) for r in range(2)]
        columns = rows_of(st_own[parity, 0:1], st_own[parity, 1:2], gain, bias, shift, *factors).T
        mean_c, rstd_c, gain_c, bias_c, shift_c = [columns[:, i : i + 1] for i in range(5)]
        for r in range(2):
            factor_c = columns[:, 5 + r : 6 + r]
            own = lat_ref[parity, r].astype(F32)
            normed_own = ((own - mean_c) * rstd_c * gain_c + bias_c + shift_c).astype(BF16).astype(F32)
            stale_own = code_ref[parity, r].astype(F32) * factor_c
            res_ref[parity, r] = ((normed_own - stale_own) / factor_c).astype(BF16)

    merge.wait_recv()
    keep_own, keep_other, sums = [], [], []
    for h in range(HEADS):
        mine, other = m_ref[h, :MINE], mrecv[:, CP + h : CP + h + 1]
        peak = jnp.maximum(mine, other)
        a, b = jnp.exp2(mine - peak), jnp.exp2(other - peak)
        keep_own.append(a)
        keep_other.append(b)
        sums.append(acc_ref[h, :MINE, 128:] * a + mrecv[:, CP + 8 + h : CP + 9 + h] * b)
    slabs = []
    for slab in range(3):
        e, o = 2 * slab, min(2 * slab + 1, HEADS - 1)

        def pick(values):
            return values[e] if e == o else jnp.where(low_half, values[e], values[o])

        own_sum = pick([acc_ref[h, :MINE, :128] for h in range(HEADS)])
        joined = own_sum * pick(keep_own) + mrecv[:, slab * 128 : (slab + 1) * 128] * pick(keep_other)
        slabs.append((joined / pick(sums)).astype(BF16))
    attended = jnp.concatenate(slabs, axis=1)
    sec[...] = (wide_ref[...].astype(F32) + dot(attended, woutp[...])).astype(BF16)

    def forward(j, source):
        return remote(
            sec.at[pl.ds(j * CELLS, CELLS)], xin.at[source], f_send.at[j], f_recv.at[source],
            worker_device(j, z, core),
        )

    for k in range(1, FRAMES):
        j = (frame + k) % FRAMES

        @pl.when(j < WORKERS)
        def _():
            forward(j, frame).start()

    band = frame // 7
    spot = frame % 7
    here = x_lo * 4 + y

    def back(target):
        return remote(
            yout.at[pl.ds(2 * target, 2)],
            got.at[pl.ds(0, 2), pl.ds(spot * CELLS, CELLS)],
            b_send.at[target],
            b_recv.at[spot],
            device(target // 4, target % 4, z, band, core),
        )

    def back_local(target):
        return pltpu.make_async_copy(
            yout.at[pl.ds(2 * target, 2)], got.at[pl.ds(0, 2), pl.ds(spot * CELLS, CELLS)], local_sem.at[1]
        )

    @pl.when(frame < WORKERS)
    def _():
        to_self = pltpu.make_async_copy(sec.at[pl.ds(frame * CELLS, CELLS)], xin.at[frame], local_sem.at[0])
        to_self.start()
        for k in range(1, FRAMES):
            forward(0, (frame + k) % FRAMES).wait_recv()
        to_self.wait()

        tile = FRAMES * 16
        row_cell = lax.broadcasted_iota(jnp.int32, (tile, tile), 0) % 16
        col_cell = lax.broadcasted_iota(jnp.int32, (tile, tile), 1) % 16
        same = row_cell == col_cell
        for part in range(CELLS // 16):
            section = xin[:, part * 16 : (part + 1) * 16, :].astype(F32)
            shifted = (section + embed_ref[...][:, None, :]).reshape(tile, C)
            mean = jnp.mean(shifted, axis=-1, keepdims=True)
            deviation = shifted - mean
            normed = (
                deviation * lax.rsqrt(jnp.mean(deviation * deviation, axis=-1, keepdims=True) + 1e-05)
            ).astype(BF16)
            proj = dot(normed, wp[...]).astype(BF16)
            mixed = []
            for slab in range(3):
                q = proj[:, slab * 128 : (slab + 1) * 128]
                k = proj[:, CP + slab * 128 : CP + (slab + 1) * 128]
                v = proj[:, 2 * CP + slab * 128 : 2 * CP + (slab + 1) * 128]
                halves = []
                for h in range(2 if slab < 2 else 1):
                    keep = low_half if h == 0 else jnp.logical_not(low_half)
                    scores = lax.dot_general(
                        jnp.where(keep, q, jnp.zeros_like(q)), k, (((1,), (1,)), ((), ())),
                        preferred_element_type=F32,
                    ) * (HEAD**-0.5)
                    scores = jnp.where(same, scores, -1e30)
                    weights = jnp.exp(scores - jnp.max(scores, axis=1, keepdims=True))
                    below = jnp.sum(weights, axis=1, keepdims=True)
                    halves.append(dot(weights.astype(BF16), v) / below)
                mixed.append(halves[0] if slab == 2 else jnp.where(low_half, halves[0], halves[1]))
            mix = jnp.concatenate(mixed, axis=1).astype(BF16)
            result = section.reshape(tile, C) + dot(mix, wtoutp[...])
            yout[:, part * 16 : (part + 1) * 16, :] = result.astype(BF16).reshape(FRAMES, 16, C)
        for k in range(8):
            target = (here + k) % 8
            stays = jnp.logical_and(k == 0, x_hi == band)

            @pl.when(stays)
            def _():
                back_local(target).start()

            @pl.when(jnp.logical_not(stays))
            def _():
                back(target).start()

    for s in range(7):
        source = x_hi * 7 + s

        @pl.when(frame == source)
        def _():
            pltpu.make_async_copy(
                yout.at[pl.ds(0, 2)], got.at[pl.ds(0, 2), pl.ds(s * CELLS, CELLS)], local_sem.at[1]
            ).wait()

        @pl.when(frame != source)
        def _():
            remote(
                yout.at[pl.ds(0, 2)], got.at[pl.ds(0, 2), pl.ds(s * CELLS, CELLS)],
                b_send.at[0], b_recv.at[s], twin,
            ).wait_recv()

    for parity in range(2):
        for r in range(2):
            out_ref[parity, r] = got[parity, r * W : (r + 1) * W, :].astype(F32).T.astype(BF16)

    for parity in range(2):
        lat_copy(parity, x_hi).wait_send()
        code_copy(parity, x_hi).wait_send()
    to_twin.wait_send()
    for copy in z_copies + side_copies + own_copies:
        copy.wait_send()
    q_copy.wait_send()
    merge.wait_send()
    for step in range(1, 4):
        for b in range(2):
            to_right(step, b).wait_send()
            to_left(step, b).wait_send()
    far_right().wait_send()
    far_left().wait_send()
    for k in range(1, FRAMES):
        j = (frame + k) % FRAMES

        @pl.when(j < WORKERS)
        def _():
            forward(j, frame).wait_send()

    @pl.when(frame < WORKERS)
    def _():
        for k in range(8):

            @pl.when(jnp.logical_not(jnp.logical_and(k == 0, x_hi == band)))
            def _():
                back((here + k) % 8).wait_send()


def frame_table():
    half = C // 2
    frequency = np.exp(-math.log(10000.0) * np.arange(half) / half)
    angles = np.arange(FRAMES)[:, None] * frequency
    return np.concatenate([np.cos(angles), np.sin(angles)], axis=-1).astype(np.float32)


VM = pl.BlockSpec(memory_space=pltpu.VMEM)
SM = pl.BlockSpec(memory_space=pltpu.SMEM)


def body(
    latent, timestep, time_weight, norm_gain, norm_bias, spatial_qkv, spatial_out,
    stale_codes, stale_exponents, temporal_qkv, temporal_out,
):
    dma = pltpu.SemaphoreType.DMA
    cells_last = jax.ShapeDtypeStruct((2, 2, C, W), BF16)
    output, residual = pl.pallas_call(
        kernel,
        out_shape=(cells_last, cells_last),
        in_specs=[SM, SM] + [VM] * 10,
        out_specs=(VM, VM),
        scratch_shapes=[
            pltpu.VMEM((2, 2, C, W), BF16),
            pltpu.VMEM((MINE, C), BF16),
            pltpu.VMEM((2, PACK, 128), BF16),
            pltpu.VMEM((ZS, 2, PACK, 128), BF16),
            pltpu.VMEM((8, C), F32),
            pltpu.VMEM((8, C), F32),
            pltpu.VMEM((8, C), F32),
            pltpu.VMEM((ZS, 8, C), F32),
            pltpu.VMEM((2, 8, C), F32),
            pltpu.VMEM((2, 8, C), F32),
            pltpu.VMEM((8, C), F32),
            pltpu.VMEM((2, 8, C), F32),
            pltpu.VMEM((256, 2 * CP), BF16),
            pltpu.VMEM((128, 2 * CP), BF16),
            pltpu.VMEM((128, 2 * CP), BF16),
            pltpu.VMEM((C, CP), BF16),
            pltpu.VMEM((CP, C), BF16),
            pltpu.VMEM((C, 3 * CP), BF16),
            pltpu.VMEM((CP, C), BF16),
            pltpu.VMEM((2, MINE, CP), BF16),
            pltpu.VMEM((HEADS, BOTH, 128), BF16),
            pltpu.VMEM((KEYS, CP), BF16),
            pltpu.VMEM((CP, KEYS), BF16),
            pltpu.VMEM((KEYS, 512), BF16),
            pltpu.VMEM((3, CP, FIRST), BF16),
            pltpu.VMEM((3, FIRST, 512), BF16),
            pltpu.VMEM((HEADS, BOTH, 128), F32),
            pltpu.VMEM((HEADS, BOTH, 256), F32),
            pltpu.VMEM((MINE, 512), F32),
            pltpu.VMEM((MINE, 512), F32),
            pltpu.VMEM((MINE, C), BF16),
            pltpu.VMEM((FRAMES, CELLS, C), BF16),
            pltpu.VMEM((FRAMES, CELLS, C), BF16),
            pltpu.VMEM((2, BAND, C), BF16),
            dma((4,)), dma((2,)), dma((2,)), dma((7,)), dma((7,)), dma((7,)), dma((7,)),
            dma((2,)), dma((ZS,)), dma((ZS,)), dma((2,)), dma((2,)), dma((2,)), dma((2,)),
            dma((2,)), dma((2,)),
            dma((FRAMES,)), dma((FRAMES,)), dma((8,)), dma((7,)), dma((2,)),
        ],
        compiler_params=pltpu.CompilerParams(
            collective_id=0, has_side_effects=True, vmem_limit_bytes=60 * 2**20
        ),
        name="block",
    )(
        timestep, stale_exponents, jnp.transpose(latent, (0, 1, 3, 2)), jnp.transpose(stale_codes, (0, 1, 3, 2)),
        time_weight, norm_gain, norm_bias, spatial_qkv, spatial_out, jnp.asarray(frame_table()),
        temporal_qkv, temporal_out,
    )
    return jnp.transpose(output, (0, 1, 3, 2)), jnp.transpose(residual, (0, 1, 3, 2))


def solution(mesh):
    placed = (
        P("frame", "patch", None, None),
        P(),
        P(),
        P(),
        P(),
        P(),
        P(),
        P("frame", "patch", None, None),
        P("frame", "patch", None),
        P(),
        P(),
    )
    return jax.shard_map(
        body,
        mesh=mesh,
        in_specs=placed,
        out_specs=(P("frame", "patch", None, None), P("frame", "patch", None, None)),
        check_vma=False,
    )
```

```python
import functools
import math

import jax
import jax.numpy as jnp
import numpy as np
from jax import lax
from jax.experimental import pallas as pl
from jax.experimental.pallas import tpu as pltpu
from jax.sharding import PartitionSpec as P

HEAD = 64
HEADS = 5
C = 320
CP = 384
GROUP_WIDTH = 10
FRAMES = 16
ROWS = 64
W = 112
BAND = 224
MINE = 2 * BAND
BOTH = 2 * MINE
ZS = 8
PACK = 560
PIECES = ((0, 288), (288, 272))
CELLS = 16
WORKERS = 14
FIRST = 512
LONG = 1280
LAST = 1024
MESH = pl.DeviceIdType.MESH
F32 = jnp.float32
BF16 = jnp.bfloat16
LOG2E = 1.4426950408889634


def dot(a, b):
    return jnp.dot(a, b, preferred_element_type=F32)


def place():
    f, p = lax.axis_index("frame"), lax.axis_index("patch")
    return f // 4, f % 4, p // 4, (p // 2) % 2, p % 2


def device(x_lo, y, z, x_hi, core):
    return (x_lo * 4 + y, z * 4 + x_hi * 2 + core)


def remote(src, dst, send, recv, target):
    return pltpu.make_async_remote_copy(
        src_ref=src, dst_ref=dst, send_sem=send, recv_sem=recv, device_id=target, device_id_type=MESH
    )


def factor_row(ex_ref, frame, row):
    lane = lax.broadcasted_iota(jnp.int32, (1, C), 1) // HEAD
    power = jnp.zeros((1, C), jnp.int32)
    for block in range(C // HEAD):
        power = jnp.where(lane == block, ex_ref[frame, row, block], power)
    out = jnp.full((1, C), 1.0, F32)
    for e in (-1, 1, 2):
        out = jnp.where(power == e, 2.0**e, out)
    return out


def rows_of(*parts):
    row = lax.broadcasted_iota(jnp.int32, (8, C), 0)
    out = jnp.zeros((8, C), F32)
    for i, part in enumerate(parts):
        out = jnp.where(row == i, part, out)
    return out


def worker_device(j, z, core):
    owner = j // 2
    return device(1 - owner // 4, owner % 4, z, j % 2, core)


def kernel(
    ts_ref, ex_ref, lat_ref, code_ref, gain_ref, bias_ref, embed_ref,
    tw_hbm, wqkv_hbm, wout_hbm, wt_hbm, wtout_hbm,
    out_ref, res_ref,
    tw_ref, wqkv_ref, wout_ref, wt_ref, wtout_ref,
    lat_in, wide_ref, stage, ring, st_mine, st_side, st_x, st_all, st_fin, st_own,
    w01, wlo, whi, wq, woutp, wp, wtoutp, qcomp, qz, kb, kt, vb, kt3, v3, m_ref, acc_ref, msend, mrecv, nsend, nrecv,
    sec, xin, yout, same_group,
    w_sems, x_send, lat_recv, code_send, code_recv, rs_right, rs_left, rr_right, rr_left,
    sx_send, sx_recv, all_send, all_recv, own_send, own_recv, q_sems, mg_send, mg_recv,
    f_send, f_recv, b_send, b_recv, local_sem,
):
    x_lo, y, z, x_hi, core = place()
    frame = 2 * ((1 - x_lo) * 4 + y) + x_hi
    twin = device(x_lo, y, z, x_hi, 1 - core)
    right = device(x_lo, y, (z + 1) % ZS, x_hi, core)
    left = device(x_lo, y, (z + ZS - 1) % ZS, x_hi, core)
    sides = [device(1 - x_lo, y, z, parity, core) for parity in range(2)]
    zcores = [
        device(x_lo, y, (z + d // 2) % ZS, x_hi, (core + d) % 2) for d in range(1, 2 * ZS)
    ]

    weight_copies = [
        pltpu.make_async_copy(src, dst, w_sems.at[i])
        for i, (src, dst) in enumerate(
            ((wqkv_hbm, wqkv_ref), (tw_hbm, tw_ref), (wout_hbm, wout_ref), (wt_hbm, wt_ref), (wtout_hbm, wtout_ref))
        )
    ]
    barrier = pltpu.get_barrier_semaphore()
    plane = [worker_device((frame + k) % FRAMES, z, core) for k in range(1, FRAMES)]
    for peer in zcores + plane:
        pl.semaphore_signal(barrier, inc=1, device_id=peer, device_id_type=MESH)
    for copy in weight_copies:
        copy.start()

    for parity in range(2):
        rows = [
            code_ref[parity, r].astype(F32).T * factor_row(ex_ref, parity, r) for r in range(2)
        ]
        for r in range(2):
            for slab in range(2):
                stage[parity, slab * BAND + r * W : slab * BAND + (r + 1) * W, :] = rows[r][
                    :, slab * 128 : (slab + 1) * 128
                ].astype(BF16)
        stage[parity, 2 * BAND :, :] = jnp.concatenate(
            [rows[0][:, 256:320], rows[1][:, 256:320]], axis=1
        ).astype(BF16)

    pl.semaphore_wait(barrier, 2 * ZS - 1 + FRAMES - 1)

    def side_copy(parity, band):
        return remote(st_side.at[parity], st_x.at[band], sx_send.at[parity], sx_recv.at[band], sides[parity])

    def lat_copy(parity, band):
        return remote(lat_ref.at[parity], lat_in.at[band], x_send.at[parity], lat_recv.at[band], sides[parity])

    def code_copy(parity, band, piece):
        rows = pl.ds(*PIECES[piece])
        return remote(
            stage.at[parity, rows], ring.at[0, band, rows],
            code_send.at[parity, piece], code_recv.at[band, piece], sides[parity],
        )

    for piece in range(2):
        for parity in range(2):
            code_copy(parity, x_hi, piece).start()
    local = []
    for parity in range(2):
        own = jnp.concatenate([lat_ref[parity, r].astype(F32).T for r in range(2)], axis=0)
        mean = jnp.sum(own, axis=0, keepdims=True) / BAND
        deviation = own - mean
        local += [mean, jnp.sum(deviation * deviation, axis=0, keepdims=True)]
    st_mine[...] = rows_of(*local)
    all_copies = [
        remote(st_mine, st_all.at[d], all_send.at[d], all_recv.at[d], zcores[d - 1]) for d in range(1, 2 * ZS)
    ]
    for copy in all_copies:
        copy.start()

    for copy in weight_copies:
        copy.wait()
    pad = jnp.zeros((C, CP - C), BF16)
    wq[...] = jnp.concatenate([wqkv_ref[:, :C], pad], axis=1)
    wkv = jnp.concatenate([wqkv_ref[:, C : 2 * C], pad, wqkv_ref[:, 2 * C :], pad], axis=1)
    w01[...] = wkv[:256]
    wlo[:64] = wkv[256:]
    wlo[64:] = jnp.zeros((64, 2 * CP), BF16)
    whi[:64] = jnp.zeros((64, 2 * CP), BF16)
    whi[64:] = wkv[256:]
    vb[:, CP:] = jnp.ones((LONG, 128), BF16)
    for i in range(3):
        v3[i, :, CP:] = jnp.ones((FIRST, 128), BF16)

    same_group[...] = (
        lax.broadcasted_iota(jnp.int32, (C, C), 0) // GROUP_WIDTH
        == lax.broadcasted_iota(jnp.int32, (C, C), 1) // GROUP_WIDTH
    ).astype(F32).astype(BF16)

    for copy in all_copies:
        copy.wait_recv()
    for parity in range(2):
        i = 2 * parity
        means = [st_mine[i : i + 1]] + [st_all[d, i : i + 1] for d in range(1, 2 * ZS)]
        total = sum(means[1:], means[0]) / (2 * ZS)
        squares = st_mine[i + 1 : i + 2]
        for d in range(1, 2 * ZS):
            squares = squares + st_all[d, i + 1 : i + 2]
        for one in means:
            squares = squares + (one - total) * (one - total) * BAND
        st_side[parity] = rows_of(total, squares)
        side_copy(parity, x_hi).start()
    for parity in range(2):
        lat_copy(parity, x_hi).start()

    def to_right(step, band):
        return remote(
            ring.at[step - 1, band], ring.at[step, band],
            rs_right.at[(step - 1) * 2 + band], rr_right.at[(step - 1) * 2 + band], right,
        )

    def to_left(step, band):
        return remote(
            ring.at[0 if step == 1 else step + 2, band], ring.at[step + 3, band],
            rs_left.at[(step - 1) * 2 + band], rr_left.at[(step - 1) * 2 + band], left,
        )

    def far_right():
        return remote(ring.at[3, 0], ring.at[7, 0], rs_right.at[6], rr_right.at[6], right)

    def far_left():
        return remote(ring.at[6, 1], ring.at[7, 1], rs_left.at[6], rr_left.at[6], left)

    def first_hop(band, piece, to, send, recv, slot):
        rows = pl.ds(*PIECES[piece])
        return remote(
            ring.at[0, band, rows], ring.at[slot, band, rows], send.at[band], recv.at[band], to
        )

    for piece in range(2):
        code_copy(0, 0, piece).wait_recv()
        first_hop(0, piece, right, rs_right, rr_right, 1).start()
        code_copy(0, 1, piece).wait_recv()
        first_hop(1, piece, left, rs_left, rr_left, 4).start()
    for piece in range(2):
        first_hop(1, piece, right, rs_right, rr_right, 1).start()
        first_hop(0, piece, left, rs_left, rr_left, 4).start()

    def project(blocks):
        x01 = jnp.concatenate(
            [jnp.concatenate([ring[s, b, :BAND], ring[s, b, BAND : 2 * BAND]], axis=1) for s, b in blocks], axis=0
        )
        tail = jnp.concatenate([ring[s, b, 2 * BAND :] for s, b in blocks], axis=0)
        low, high = dot(tail, wlo[...]), dot(tail, whi[...])
        rest = []
        for i in range(len(blocks)):
            rest += [low[i * W : (i + 1) * W], high[i * W : (i + 1) * W]]
        both = (dot(x01, w01[...]) + jnp.concatenate(rest, axis=0)).astype(BF16)
        return both[:, :CP], both[:, CP:]

    stale_k, stale_v = project([(0, 0), (0, 1)])

    woutp[:C] = wout_ref[...]
    woutp[C:] = jnp.zeros((CP - C, C), BF16)
    wp[...] = jnp.concatenate([wt_ref[:, :C], pad, wt_ref[:, C : 2 * C], pad, wt_ref[:, 2 * C :], pad], axis=1)
    wtoutp[:C] = wtout_ref[...]
    wtoutp[C:] = jnp.zeros((CP - C, C), BF16)

    lane = lax.broadcasted_iota(jnp.int32, (1, C), 1)
    half = C // 2
    index = jnp.where(lane < half, lane, lane - half).astype(F32)
    angle = ts_ref[0].astype(F32) * jnp.exp(-math.log(10000.0) * index / half)
    embed = jnp.where(lane < half, jnp.cos(angle), jnp.sin(angle)).astype(BF16)
    shift = dot(jnp.broadcast_to(embed, (16, C)), tw_ref[...])[0:1]
    gain = gain_ref[...].reshape(1, C)
    bias = bias_ref[...].reshape(1, C)

    for band in range(2):
        side_copy(0, band).wait_recv()
    total = (st_x[0, 0:1] + st_x[1, 0:1]) * 0.5
    delta = st_x[0, 0:1] - st_x[1, 0:1]
    cells = ROWS * W
    squares = st_x[0, 1:2] + st_x[1, 1:2] + delta * delta * (cells / 4)

    def group_sum(row):
        high = row.astype(BF16)
        left_over = row - high.astype(F32)
        middle = left_over.astype(BF16)
        low = (left_over - middle.astype(F32)).astype(BF16)
        sums = dot(
            jnp.concatenate([jnp.broadcast_to(part, (16, C)) for part in (high, middle, low)], axis=0),
            same_group[...],
        )
        return sums[0:1] + sums[16:17] + sums[32:33]

    group_mean = group_sum(total) / GROUP_WIDTH
    off = total - group_mean
    group_var = group_sum(squares + off * off * cells) / (cells * GROUP_WIDTH)
    rstd = lax.rsqrt(group_var + 1e-05)
    st_fin[...] = rows_of(group_mean, rstd)
    own_copies = [
        remote(st_fin, st_own.at[x_hi], own_send.at[i], own_recv.at[x_hi], sides[i]) for i in range(2)
    ]
    for copy in own_copies:
        copy.start()

    for band in range(2):
        lat_copy(0, band).wait_recv()
        for r in range(2):
            wide_ref[band * BAND + r * W : band * BAND + (r + 1) * W] = (
                lat_in[band, r].astype(F32).T.astype(BF16)
            )
    wide = wide_ref[...].astype(F32)
    normed = ((wide - group_mean) * rstd * gain + bias + shift).astype(BF16)
    qcomp[0] = (dot(normed, wq[...]) * (HEAD**-0.5 * LOG2E)).astype(BF16)
    q_copy = remote(qcomp.at[0], qcomp.at[1], q_sems.at[0], q_sems.at[1], twin)
    q_copy.start()
    fresh = (dot(normed[:, :256], w01[...]) + dot(normed[:, 256:], wlo[:64])).astype(BF16)
    fresh_k, fresh_v = fresh[:, :CP], fresh[:, CP:]

    def pass_right(step, band):
        to_right(step, band).wait_recv()
        to_right(step + 1, band).start()

    def pass_left(step, band):
        to_left(step, band).wait_recv()
        to_left(step + 1, band).start()

    pass_right(1, 0)
    pass_left(1, 1)
    near_k, near_v = project([(1, 0), (4, 1)])
    lead = FIRST - MINE
    rest = LONG - FIRST
    own_k = [
        jnp.concatenate([fresh_k[:BAND], stale_k[BAND:], near_k[:lead]], axis=0),
        jnp.concatenate([stale_k[:BAND], fresh_k[BAND:], near_k[:lead]], axis=0),
        jnp.concatenate([stale_k, near_k[:lead]], axis=0),
    ]
    own_v = [
        jnp.concatenate([fresh_v[:BAND], stale_v[BAND:], near_v[:lead]], axis=0),
        jnp.concatenate([stale_v[:BAND], fresh_v[BAND:], near_v[:lead]], axis=0),
        jnp.concatenate([stale_v, near_v[:lead]], axis=0),
    ]
    for i in range(3):
        kt3[i] = own_k[i].T
        v3[i, :, :CP] = own_v[i]

    lane128 = lax.broadcasted_iota(jnp.int32, (1, 128), 1)
    low_half = lane128 < HEAD
    q_copy.wait_recv()
    for who in range(2):
        for h in range(HEADS):
            slab = qcomp[who, :, (h // 2) * 128 : (h // 2) * 128 + 128]
            keep = low_half if h % 2 == 0 else jnp.logical_not(low_half)
            slab = jnp.where(keep, slab, jnp.zeros_like(slab))
            for b in range(2):
                qz[h, b * MINE + who * BAND : b * MINE + (who + 1) * BAND, :] = slab[b * BAND : (b + 1) * BAND]

    pass_right(1, 1)
    pass_left(1, 0)
    next_k, next_v = project([(1, 1), (4, 0)])
    first_k = jnp.concatenate([near_k, next_k], axis=0)
    first_v = jnp.concatenate([near_v, next_v], axis=0)
    kt[:, :rest] = first_k[lead : lead + rest].T
    vb[:rest, :CP] = first_v[lead : lead + rest]

    def attend(items, scores_of, values_of, first, between):
        scores = scores_of(*items[0])
        for n, (h, a, b) in enumerate(items):
            following = scores_of(*items[n + 1]) if n + 1 < len(items) else None
            peak = jnp.max(scores, axis=1, keepdims=True)
            if not first:
                old = m_ref[h, a:b][:, :1]
                peak = jnp.maximum(old, peak)
            weights = jnp.exp2(scores - peak).astype(BF16)
            m_ref[h, a:b] = jnp.broadcast_to(peak, (b - a, 128))
            if first:
                acc_ref[h, a:b] = values_of(h, weights)
            else:
                acc_ref[h, a:b] = acc_ref[h, a:b] * jnp.exp2(old - peak) + values_of(h, weights)
            scores = following
            if n in between:
                between[n]()

    def all_heads(a, b):
        return [(h, a, b) for h in range(HEADS)]

    parts = ((0, 0, BAND), (2, BAND, MINE), (1, MINE, MINE + BAND), (2, MINE + BAND, BOTH))

    def own_scores(h, start, stop):
        s = h // 2 * 128
        own = jnp.concatenate([dot(qz[h, a:b], kt3[i, s : s + 128]) for i, a, b in parts], axis=0)
        return jnp.concatenate([own, dot(qz[h, start:stop], kt[s : s + 128, :rest])], axis=1)

    def own_values(h, weights):
        s = h // 2 * 128
        own = jnp.concatenate(
            [
                dot(weights[a:b, :FIRST], jnp.concatenate([v3[i, :, s : s + 128], v3[i, :, CP:]], axis=1))
                for i, a, b in parts
            ],
            axis=0,
        )
        return own + dot(weights[:, FIRST:], jnp.concatenate([vb[:rest, s : s + 128], vb[:rest, CP:]], axis=1))

    def second_first():
        pass_right(2, 0)
        pass_left(2, 1)

    def second_last():
        pass_right(2, 1)
        pass_left(2, 0)

    attend(all_heads(0, BOTH), own_scores, own_values, True, {0: second_first, 2: second_last})

    def chunk(keys, items, between):
        def scores_of(h, a, b):
            s = h // 2 * 128
            return dot(qz[h, a:b], kt[s : s + 128, :keys])

        def values_of(h, weights):
            s = h // 2 * 128
            return dot(weights, jnp.concatenate([vb[:keys, s : s + 128], vb[:keys, CP:]], axis=1))

        attend(items, scores_of, values_of, False, between)

    left_k, left_v = first_k[lead + rest :], first_v[lead + rest :]
    count = left_k.shape[0]
    kb[:count] = left_k
    vb[:count, :CP] = left_v
    k, v = project([(2, 0), (5, 1), (2, 1), (5, 0)])
    kb[count : count + BOTH] = k
    vb[count : count + BOTH, :CP] = v
    count += BOTH
    to_right(3, 0).wait_recv()
    far_right().start()
    to_left(3, 1).wait_recv()
    far_left().start()
    k, v = project([(3, 0), (6, 1)])
    kb[count:] = k[: LONG - count]
    vb[count:, :CP] = v[: LONG - count]
    left_k, left_v = k[LONG - count :], v[LONG - count :]
    kt[...] = kb[...].T
    chunk(LONG, all_heads(0, BOTH), {})

    count = left_k.shape[0]
    kb[:count] = left_k
    vb[:count, :CP] = left_v
    to_right(3, 1).wait_recv()
    to_left(3, 0).wait_recv()
    k, v = project([(3, 1), (6, 0)])
    kb[count : count + MINE] = k
    vb[count : count + MINE, :CP] = v
    count += MINE
    far_right().wait_recv()
    far_left().wait_recv()
    k, v = project([(7, 0), (7, 1)])
    kb[count:LAST] = k
    vb[count:LAST, :CP] = v
    kt[:, :LAST] = kb[:LAST].T

    def merge(b):
        return [
            remote(msend.at[b], mrecv.at[b], mg_send.at[b, 0], mg_recv.at[b, 0], twin),
            remote(nsend.at[b], nrecv.at[b], mg_send.at[b, 1], mg_recv.at[b, 1], twin),
        ]

    def give(b):
        rows = slice(b * MINE + BAND, (b + 1) * MINE)
        notes = jnp.zeros((BAND, 128), F32)
        for h in range(HEADS):
            notes = jnp.where(lane128 == h, m_ref[h, rows], notes)
            notes = jnp.where(lane128 == 8 + h, acc_ref[h, rows, 128:], notes)
        for slab in range(3):
            one = acc_ref[2 * slab, rows, :128]
            if slab < 2:
                one = jnp.where(low_half, one, acc_ref[2 * slab + 1, rows, :128])
            msend[b, :, slab * 128 : (slab + 1) * 128] = one.astype(BF16)
        nsend[b] = notes
        for copy in merge(b):
            copy.start()

    def forward(b, j, source):
        return remote(
            sec.at[b, pl.ds(j * CELLS, CELLS)], xin.at[b, source], f_send.at[b, j], f_recv.at[b, source],
            worker_device(j, z, core),
        )

    def to_self(b):
        return pltpu.make_async_copy(
            sec.at[b, pl.ds(frame * CELLS, CELLS)], xin.at[b, frame], local_sem.at[b]
        )

    def take(b):
        rows = slice(b * MINE, b * MINE + BAND)
        for copy in merge(b):
            copy.wait_recv()
        keep_own, keep_other, sums = [], [], []
        for h in range(HEADS):
            mine, other = m_ref[h, rows], nrecv[b, :, h : h + 1]
            peak = jnp.maximum(mine, other)
            own_part, other_part = jnp.exp2(mine - peak), jnp.exp2(other - peak)
            keep_own.append(own_part)
            keep_other.append(other_part)
            sums.append(
                acc_ref[h, rows, 128:] * own_part + nrecv[b, :, 8 + h : 9 + h] * other_part
            )
        slabs = []
        for slab in range(3):
            e, o = 2 * slab, min(2 * slab + 1, HEADS - 1)

            def pick(values):
                return values[e] if e == o else jnp.where(low_half, values[e], values[o])

            own_sum = pick([acc_ref[h, rows, :128] for h in range(HEADS)])
            joined = own_sum * pick(keep_own) + mrecv[b, :, slab * 128 : (slab + 1) * 128].astype(F32) * pick(keep_other)
            slabs.append((joined / pick(sums)).astype(BF16))
        attended = jnp.concatenate(slabs, axis=1)
        sec[b] = (wide_ref[b * BAND : (b + 1) * BAND].astype(F32) + dot(attended, woutp[...])).astype(BF16)
        for k in range(1, FRAMES):
            j = (frame + k) % FRAMES

            @pl.when(j < WORKERS)
            def _():
                forward(b, j, frame).start()

        @pl.when(frame < WORKERS)
        def _():
            to_self(b).start()

    chunk(LAST, all_heads(0, MINE), {})
    give(0)
    chunk(LAST, all_heads(MINE, BOTH), {2: lambda: take(0)})
    give(1)

    for parity in range(2):
        remote(st_fin, st_own.at[parity], own_send.at[0], own_recv.at[parity], sides[0]).wait_recv()
        factors = [factor_row(ex_ref, parity, r) for r in range(2)]
        columns = rows_of(st_own[parity, 0:1], st_own[parity, 1:2], gain, bias, shift, *factors).T
        mean_c, rstd_c, gain_c, bias_c, shift_c = [columns[:, i : i + 1] for i in range(5)]
        for r in range(2):
            factor_c = columns[:, 5 + r : 6 + r]
            own = lat_ref[parity, r].astype(F32)
            normed_own = ((own - mean_c) * rstd_c * gain_c + bias_c + shift_c).astype(BF16).astype(F32)
            stale_own = code_ref[parity, r].astype(F32) * factor_c
            res_ref[parity, r] = ((normed_own - stale_own) / factor_c).astype(BF16)

    take(1)

    here = x_lo * 4 + y

    def back(b, target):
        return remote(
            yout.at[b, pl.ds(2 * target, 2)],
            out_ref.at[pl.ds(0, 2), pl.ds(frame * CELLS, CELLS)],
            b_send.at[b, target],
            b_recv.at[frame],
            device(target // 4, target % 4, z, b, core),
        )

    @pl.when(frame < WORKERS)
    def _():
        tile = FRAMES * CELLS
        row_cell = lax.broadcasted_iota(jnp.int32, (tile, tile), 0) % CELLS
        col_cell = lax.broadcasted_iota(jnp.int32, (tile, tile), 1) % CELLS
        same = row_cell == col_cell
        for b in range(2):
            for k in range(1, FRAMES):
                forward(b, 0, (frame + k) % FRAMES).wait_recv()
            to_self(b).wait()
            section = xin[b].astype(F32)
            shifted = (section + embed_ref[...][:, None, :]).reshape(tile, C)
            mean = jnp.mean(shifted, axis=-1, keepdims=True)
            deviation = shifted - mean
            normed_t = (
                deviation * lax.rsqrt(jnp.mean(deviation * deviation, axis=-1, keepdims=True) + 1e-05)
            ).astype(BF16)
            proj = dot(normed_t, wp[...]).astype(BF16)
            mixed = []
            for slab in range(3):
                q = proj[:, slab * 128 : (slab + 1) * 128]
                k = proj[:, CP + slab * 128 : CP + (slab + 1) * 128]
                v = proj[:, 2 * CP + slab * 128 : 2 * CP + (slab + 1) * 128]
                halves = []
                for h in range(2 if slab < 2 else 1):
                    keep = low_half if h == 0 else jnp.logical_not(low_half)
                    scores = lax.dot_general(
                        jnp.where(keep, q, jnp.zeros_like(q)), k, (((1,), (1,)), ((), ())),
                        preferred_element_type=F32,
                    ) * (HEAD**-0.5)
                    scores = jnp.where(same, scores, -1e30)
                    weights = jnp.exp(scores - jnp.max(scores, axis=1, keepdims=True))
                    below = jnp.sum(weights, axis=1, keepdims=True)
                    halves.append(dot(weights.astype(BF16), v) / below)
                mixed.append(halves[0] if slab == 2 else jnp.where(low_half, halves[0], halves[1]))
            mix = jnp.concatenate(mixed, axis=1).astype(BF16)
            result = section.reshape(tile, C) + dot(mix, wtoutp[...])
            yout[b] = result.astype(BF16).reshape(FRAMES, CELLS, C)
            for k in range(8):
                stays = jnp.logical_and(k == 0, x_hi == b)

                @pl.when(stays)
                def _():
                    pltpu.make_async_copy(
                        yout.at[b, pl.ds(2 * here, 2)],
                        out_ref.at[pl.ds(0, 2), pl.ds(frame * CELLS, CELLS)],
                        local_sem.at[2],
                    ).start()

                @pl.when(jnp.logical_not(stays))
                def _():
                    back(b, (here + k) % 8).start()

    for s in range(WORKERS):

        @pl.when(frame == s)
        def _():
            pltpu.make_async_copy(
                yout.at[0, pl.ds(0, 2)], out_ref.at[pl.ds(0, 2), pl.ds(s * CELLS, CELLS)], local_sem.at[2]
            ).wait()

        @pl.when(frame != s)
        def _():
            remote(
                yout.at[0, pl.ds(0, 2)], out_ref.at[pl.ds(0, 2), pl.ds(s * CELLS, CELLS)],
                b_send.at[0, 0], b_recv.at[s], twin,
            ).wait_recv()

    for parity in range(2):
        for send in (side_copy, lat_copy):
            send(parity, x_hi).wait_send()
        for piece in range(2):
            code_copy(parity, x_hi, piece).wait_send()
    for copy in all_copies + own_copies:
        copy.wait_send()
    q_copy.wait_send()
    for step in range(1, 4):
        for b in range(2):
            to_right(step, b).wait_send()
            to_left(step, b).wait_send()
    far_right().wait_send()
    far_left().wait_send()
    for b in range(2):
        for copy in merge(b):
            copy.wait_send()
        for k in range(1, FRAMES):
            j = (frame + k) % FRAMES

            @pl.when(j < WORKERS)
            def _():
                forward(b, j, frame).wait_send()

    @pl.when(frame < WORKERS)
    def _():
        for b in range(2):
            for k in range(8):

                @pl.when(jnp.logical_not(jnp.logical_and(k == 0, x_hi == b)))
                def _():
                    back(b, (here + k) % 8).wait_send()


def frame_table():
    half = C // 2
    frequency = np.exp(-math.log(10000.0) * np.arange(half) / half)
    angles = np.arange(FRAMES)[:, None] * frequency
    return np.concatenate([np.cos(angles), np.sin(angles)], axis=-1).astype(np.float32)


VM = pl.BlockSpec(memory_space=pltpu.VMEM)
SM = pl.BlockSpec(memory_space=pltpu.SMEM)
HBM = pl.BlockSpec(memory_space=pl.ANY)


def body(
    latent, timestep, time_weight, norm_gain, norm_bias, spatial_qkv, spatial_out,
    stale_codes, stale_exponents, temporal_qkv, temporal_out,
):
    dma = pltpu.SemaphoreType.DMA
    output, residual = pl.pallas_call(
        kernel,
        out_shape=(pltpu.VMEM((2, BAND, C), BF16), pltpu.VMEM((2, 2, C, W), BF16)),
        in_specs=[SM, SM] + [VM] * 5 + [HBM] * 5,
        out_specs=(VM, VM),
        scratch_shapes=[
            pltpu.VMEM((C, C), BF16),
            pltpu.VMEM((C, 3 * C), BF16),
            pltpu.VMEM((C, C), BF16),
            pltpu.VMEM((C, 3 * C), BF16),
            pltpu.VMEM((C, C), BF16),
            pltpu.VMEM((2, 2, C, W), BF16),
            pltpu.VMEM((MINE, C), BF16),
            pltpu.VMEM((2, PACK, 128), BF16),
            pltpu.VMEM((ZS, 2, PACK, 128), BF16),
            pltpu.VMEM((8, C), F32),
            pltpu.VMEM((2, 8, C), F32),
            pltpu.VMEM((2, 8, C), F32),
            pltpu.VMEM((2 * ZS, 8, C), F32),
            pltpu.VMEM((8, C), F32),
            pltpu.VMEM((2, 8, C), F32),
            pltpu.VMEM((256, 2 * CP), BF16),
            pltpu.VMEM((128, 2 * CP), BF16),
            pltpu.VMEM((128, 2 * CP), BF16),
            pltpu.VMEM((C, CP), BF16),
            pltpu.VMEM((CP, C), BF16),
            pltpu.VMEM((C, 3 * CP), BF16),
            pltpu.VMEM((CP, C), BF16),
            pltpu.VMEM((2, MINE, CP), BF16),
            pltpu.VMEM((HEADS, BOTH, 128), BF16),
            pltpu.VMEM((LONG, CP), BF16),
            pltpu.VMEM((CP, LONG), BF16),
            pltpu.VMEM((LONG, 512), BF16),
            pltpu.VMEM((3, CP, FIRST), BF16),
            pltpu.VMEM((3, FIRST, 512), BF16),
            pltpu.VMEM((HEADS, BOTH, 128), F32),
            pltpu.VMEM((HEADS, BOTH, 256), F32),
            pltpu.VMEM((2, BAND, CP), BF16),
            pltpu.VMEM((2, BAND, CP), BF16),
            pltpu.VMEM((2, BAND, 128), F32),
            pltpu.VMEM((2, BAND, 128), F32),
            pltpu.VMEM((2, BAND, C), BF16),
            pltpu.VMEM((2, FRAMES, CELLS, C), BF16),
            pltpu.VMEM((2, FRAMES, CELLS, C), BF16),
            pltpu.VMEM((C, C), BF16),
            dma((5,)), dma((2,)), dma((2,)), dma((2, 2)), dma((2, 2)), dma((7,)), dma((7,)), dma((7,)), dma((7,)),
            dma((2,)), dma((2,)), dma((2 * ZS,)), dma((2 * ZS,)), dma((2,)), dma((2,)), dma((2,)),
            dma((2, 2)), dma((2, 2)),
            dma((2, FRAMES)), dma((2, FRAMES)), dma((2, 8)), dma((WORKERS,)), dma((3,)),
        ],
        compiler_params=pltpu.CompilerParams(
            collective_id=0, has_side_effects=True, vmem_limit_bytes=60 * 2**20
        ),
        name="block",
    )(
        timestep, stale_exponents, jnp.transpose(latent, (0, 1, 3, 2)), jnp.transpose(stale_codes, (0, 1, 3, 2)),
        norm_gain, norm_bias, jnp.asarray(frame_table()),
        time_weight, spatial_qkv, spatial_out, temporal_qkv, temporal_out,
    )
    return output.reshape(2, 2, W, C), jnp.transpose(residual, (0, 1, 3, 2))


def solution(mesh):
    placed = (
        P("frame", "patch", None, None),
        P(),
        P(),
        P(),
        P(),
        P(),
        P(),
        P("frame", "patch", None, None),
        P("frame", "patch", None),
        P(),
        P(),
    )
    return jax.shard_map(
        body,
        mesh=mesh,
        in_specs=placed,
        out_specs=(P("frame", "patch", None, None), P("frame", "patch", None, None)),
        check_vma=False,
    )
```

```python
import functools
import math

import jax
import jax.numpy as jnp
import numpy as np
from jax import lax
from jax.experimental import pallas as pl
from jax.experimental.pallas import tpu as pltpu
from jax.sharding import PartitionSpec as P

HEAD = 64
HEADS = 5
C = 320
CP = 384
GROUP_WIDTH = 10
FRAMES = 16
ROWS = 64
W = 112
BAND = 224
MINE = 2 * BAND
BOTH = 2 * MINE
ZS = 8
PACK = 560
PIECES = ((0, 288), (288, 272))
CELLS = 16
WORKERS = 14
FIRST = 512
LONG = 1280
LAST = 1024
MESH = pl.DeviceIdType.MESH
F32 = jnp.float32
BF16 = jnp.bfloat16
LOG2E = 1.4426950408889634


def dot(a, b):
    return jnp.dot(a, b, preferred_element_type=F32)


def place():
    f, p = lax.axis_index("frame"), lax.axis_index("patch")
    return f // 4, f % 4, p // 4, (p // 2) % 2, p % 2


def device(x_lo, y, z, x_hi, core):
    return (x_lo * 4 + y, z * 4 + x_hi * 2 + core)


def remote(src, dst, send, recv, target):
    return pltpu.make_async_remote_copy(
        src_ref=src, dst_ref=dst, send_sem=send, recv_sem=recv, device_id=target, device_id_type=MESH
    )


def factor_row(ex_ref, frame, row):
    lane = lax.broadcasted_iota(jnp.int32, (1, C), 1) // HEAD
    power = jnp.zeros((1, C), jnp.int32)
    for block in range(C // HEAD):
        power = jnp.where(lane == block, ex_ref[frame, row, block], power)
    out = jnp.full((1, C), 1.0, F32)
    for e in (-1, 1, 2):
        out = jnp.where(power == e, 2.0**e, out)
    return out


def rows_of(*parts):
    row = lax.broadcasted_iota(jnp.int32, (8, C), 0)
    out = jnp.zeros((8, C), F32)
    for i, part in enumerate(parts):
        out = jnp.where(row == i, part, out)
    return out


def worker_device(j, z, core):
    owner = j // 2
    return device(1 - owner // 4, owner % 4, z, j % 2, core)


def kernel(
    ts_ref, ex_ref, lat_ref, code_ref, gain_ref, bias_ref, embed_ref,
    tw_hbm, wqkv_hbm, wout_hbm, wt_hbm, wtout_hbm,
    out_ref, res_ref,
    tw_ref, wqkv_ref, wout_ref, wt_ref, wtout_ref,
    lat_in, wide_ref, stage, ring, st_mine, st_side, st_x, st_all, st_fin, st_own,
    w01, wlo, whi, wq, woutp, wp, wtoutp, qcomp, qz, kb, kt, vb, kt3, v3, m_ref, acc_ref, msend, mrecv, nsend, nrecv,
    sec, xin, yout, same_group,
    w_sems, x_send, lat_recv, code_send, code_recv, rs_right, rs_left, rr_right, rr_left,
    sx_send, sx_recv, all_send, all_recv, own_send, own_recv, q_sems, mg_send, mg_recv,
    f_send, f_recv, b_send, b_recv, local_sem,
):
    x_lo, y, z, x_hi, core = place()
    frame = 2 * ((1 - x_lo) * 4 + y) + x_hi
    twin = device(x_lo, y, z, x_hi, 1 - core)
    right = device(x_lo, y, (z + 1) % ZS, x_hi, core)
    left = device(x_lo, y, (z + ZS - 1) % ZS, x_hi, core)
    sides = [device(1 - x_lo, y, z, parity, core) for parity in range(2)]
    zcores = [
        device(x_lo, y, (z + d // 2) % ZS, x_hi, (core + d) % 2) for d in range(1, 2 * ZS)
    ]

    weight_copies = [
        pltpu.make_async_copy(src, dst, w_sems.at[i])
        for i, (src, dst) in enumerate(
            ((wqkv_hbm, wqkv_ref), (tw_hbm, tw_ref), (wout_hbm, wout_ref), (wt_hbm, wt_ref), (wtout_hbm, wtout_ref))
        )
    ]
    barrier = pltpu.get_barrier_semaphore()
    plane = [worker_device((frame + k) % FRAMES, z, core) for k in range(1, FRAMES)]
    for peer in zcores + plane:
        pl.semaphore_signal(barrier, inc=1, device_id=peer, device_id_type=MESH)
    for copy in weight_copies:
        copy.start()

    for parity in range(2):
        rows = [
            code_ref[parity, r].astype(F32).T * factor_row(ex_ref, parity, r) for r in range(2)
        ]
        for r in range(2):
            for slab in range(2):
                stage[parity, slab * BAND + r * W : slab * BAND + (r + 1) * W, :] = rows[r][
                    :, slab * 128 : (slab + 1) * 128
                ].astype(BF16)
        stage[parity, 2 * BAND :, :] = jnp.concatenate(
            [rows[0][:, 256:320], rows[1][:, 256:320]], axis=1
        ).astype(BF16)

    pl.semaphore_wait(barrier, 2 * ZS - 1 + FRAMES - 1)

    def side_copy(parity, band):
        return remote(st_side.at[parity], st_x.at[band], sx_send.at[parity], sx_recv.at[band], sides[parity])

    def lat_copy(parity, band):
        return remote(lat_ref.at[parity], lat_in.at[band], x_send.at[parity], lat_recv.at[band], sides[parity])

    def code_copy(parity, band, piece):
        rows = pl.ds(*PIECES[piece])
        return remote(
            stage.at[parity, rows], ring.at[0, band, rows],
            code_send.at[parity, piece], code_recv.at[band, piece], sides[parity],
        )

    for piece in range(2):
        for parity in range(2):
            code_copy(parity, x_hi, piece).start()
    local = []
    for parity in range(2):
        own = jnp.concatenate([lat_ref[parity, r].astype(F32).T for r in range(2)], axis=0)
        mean = jnp.sum(own, axis=0, keepdims=True) / BAND
        deviation = own - mean
        local += [mean, jnp.sum(deviation * deviation, axis=0, keepdims=True)]
    st_mine[...] = rows_of(*local)
    all_copies = [
        remote(st_mine, st_all.at[d], all_send.at[d], all_recv.at[d], zcores[d - 1]) for d in range(1, 2 * ZS)
    ]
    for copy in all_copies:
        copy.start()

    for copy in weight_copies:
        copy.wait()
    pad = jnp.zeros((C, CP - C), BF16)
    wq[...] = jnp.concatenate([wqkv_ref[:, :C], pad], axis=1)
    wkv = jnp.concatenate([wqkv_ref[:, C : 2 * C], pad, wqkv_ref[:, 2 * C :], pad], axis=1)
    w01[...] = wkv[:256]
    wlo[:64] = wkv[256:]
    wlo[64:] = jnp.zeros((64, 2 * CP), BF16)
    whi[:64] = jnp.zeros((64, 2 * CP), BF16)
    whi[64:] = wkv[256:]
    vb[:, CP:] = jnp.ones((LONG, 128), BF16)
    for i in range(3):
        v3[i, :, CP:] = jnp.ones((FIRST, 128), BF16)

    same_group[...] = (
        lax.broadcasted_iota(jnp.int32, (C, C), 0) // GROUP_WIDTH
        == lax.broadcasted_iota(jnp.int32, (C, C), 1) // GROUP_WIDTH
    ).astype(F32).astype(BF16)

    for copy in all_copies:
        copy.wait_recv()
    for parity in range(2):
        i = 2 * parity
        means = [st_mine[i : i + 1]] + [st_all[d, i : i + 1] for d in range(1, 2 * ZS)]
        total = sum(means[1:], means[0]) / (2 * ZS)
        squares = st_mine[i + 1 : i + 2]
        for d in range(1, 2 * ZS):
            squares = squares + st_all[d, i + 1 : i + 2]
        for one in means:
            squares = squares + (one - total) * (one - total) * BAND
        st_side[parity] = rows_of(total, squares)
        side_copy(parity, x_hi).start()
    for parity in range(2):
        lat_copy(parity, x_hi).start()

    def to_right(step, band):
        return remote(
            ring.at[step - 1, band], ring.at[step, band],
            rs_right.at[(step - 1) * 2 + band], rr_right.at[(step - 1) * 2 + band], right,
        )

    def to_left(step, band):
        return remote(
            ring.at[0 if step == 1 else step + 2, band], ring.at[step + 3, band],
            rs_left.at[(step - 1) * 2 + band], rr_left.at[(step - 1) * 2 + band], left,
        )

    def far_right():
        return remote(ring.at[3, 0], ring.at[7, 0], rs_right.at[6], rr_right.at[6], right)

    def far_left():
        return remote(ring.at[6, 1], ring.at[7, 1], rs_left.at[6], rr_left.at[6], left)

    def first_hop(band, piece, to, send, recv, slot):
        rows = pl.ds(*PIECES[piece])
        return remote(
            ring.at[0, band, rows], ring.at[slot, band, rows], send.at[band], recv.at[band], to
        )

    for piece in range(2):
        code_copy(0, 0, piece).wait_recv()
        first_hop(0, piece, right, rs_right, rr_right, 1).start()
        code_copy(0, 1, piece).wait_recv()
        first_hop(1, piece, left, rs_left, rr_left, 4).start()
    for piece in range(2):
        first_hop(1, piece, right, rs_right, rr_right, 1).start()
        first_hop(0, piece, left, rs_left, rr_left, 4).start()

    def project(blocks):
        x01 = jnp.concatenate(
            [jnp.concatenate([ring[s, b, :BAND], ring[s, b, BAND : 2 * BAND]], axis=1) for s, b in blocks], axis=0
        )
        tail = jnp.concatenate([ring[s, b, 2 * BAND :] for s, b in blocks], axis=0)
        low, high = dot(tail, wlo[...]), dot(tail, whi[...])
        rest = []
        for i in range(len(blocks)):
            rest += [low[i * W : (i + 1) * W], high[i * W : (i + 1) * W]]
        both = (dot(x01, w01[...]) + jnp.concatenate(rest, axis=0)).astype(BF16)
        return both[:, :CP], both[:, CP:]

    stale_k, stale_v = project([(0, 0), (0, 1)])

    woutp[:C] = wout_ref[...]
    woutp[C:] = jnp.zeros((CP - C, C), BF16)
    wp[...] = jnp.concatenate([wt_ref[:, :C], pad, wt_ref[:, C : 2 * C], pad, wt_ref[:, 2 * C :], pad], axis=1)
    wtoutp[:C] = wtout_ref[...]
    wtoutp[C:] = jnp.zeros((CP - C, C), BF16)

    lane = lax.broadcasted_iota(jnp.int32, (1, C), 1)
    half = C // 2
    index = jnp.where(lane < half, lane, lane - half).astype(F32)
    angle = ts_ref[0].astype(F32) * jnp.exp(-math.log(10000.0) * index / half)
    embed = jnp.where(lane < half, jnp.cos(angle), jnp.sin(angle)).astype(BF16)
    shift = dot(jnp.broadcast_to(embed, (16, C)), tw_ref[...])[0:1]
    gain = gain_ref[...].reshape(1, C)
    bias = bias_ref[...].reshape(1, C)

    for band in range(2):
        side_copy(0, band).wait_recv()
    total = (st_x[0, 0:1] + st_x[1, 0:1]) * 0.5
    delta = st_x[0, 0:1] - st_x[1, 0:1]
    cells = ROWS * W
    squares = st_x[0, 1:2] + st_x[1, 1:2] + delta * delta * (cells / 4)

    def group_sum(row):
        high = row.astype(BF16)
        left_over = row - high.astype(F32)
        middle = left_over.astype(BF16)
        low = (left_over - middle.astype(F32)).astype(BF16)
        sums = dot(
            jnp.concatenate([jnp.broadcast_to(part, (16, C)) for part in (high, middle, low)], axis=0),
            same_group[...],
        )
        return sums[0:1] + sums[16:17] + sums[32:33]

    group_mean = group_sum(total) / GROUP_WIDTH
    off = total - group_mean
    group_var = group_sum(squares + off * off * cells) / (cells * GROUP_WIDTH)
    rstd = lax.rsqrt(group_var + 1e-05)
    st_fin[...] = rows_of(group_mean, rstd)
    own_copies = [
        remote(st_fin, st_own.at[x_hi], own_send.at[i], own_recv.at[x_hi], sides[i]) for i in range(2)
    ]
    for copy in own_copies:
        copy.start()

    for band in range(2):
        lat_copy(0, band).wait_recv()
        for r in range(2):
            wide_ref[band * BAND + r * W : band * BAND + (r + 1) * W] = (
                lat_in[band, r].astype(F32).T.astype(BF16)
            )
    wide = wide_ref[...].astype(F32)
    normed = ((wide - group_mean) * rstd * gain + bias + shift).astype(BF16)
    qcomp[0] = (dot(normed, wq[...]) * (HEAD**-0.5 * LOG2E)).astype(BF16)
    q_copy = remote(qcomp.at[0], qcomp.at[1], q_sems.at[0], q_sems.at[1], twin)
    q_copy.start()
    fresh = (dot(normed[:, :256], w01[...]) + dot(normed[:, 256:], wlo[:64])).astype(BF16)
    fresh_k, fresh_v = fresh[:, :CP], fresh[:, CP:]

    def pass_right(step, band):
        to_right(step, band).wait_recv()
        to_right(step + 1, band).start()

    def pass_left(step, band):
        to_left(step, band).wait_recv()
        to_left(step + 1, band).start()

    pass_right(1, 0)
    pass_left(1, 1)
    near_k, near_v = project([(1, 0), (4, 1)])
    lead = FIRST - MINE
    rest = LONG - FIRST
    own_k = [
        jnp.concatenate([fresh_k[:BAND], stale_k[BAND:], near_k[:lead]], axis=0),
        jnp.concatenate([stale_k[:BAND], fresh_k[BAND:], near_k[:lead]], axis=0),
        jnp.concatenate([stale_k, near_k[:lead]], axis=0),
    ]
    own_v = [
        jnp.concatenate([fresh_v[:BAND], stale_v[BAND:], near_v[:lead]], axis=0),
        jnp.concatenate([stale_v[:BAND], fresh_v[BAND:], near_v[:lead]], axis=0),
        jnp.concatenate([stale_v, near_v[:lead]], axis=0),
    ]
    for i in range(3):
        kt3[i] = own_k[i].T
        v3[i, :, :CP] = own_v[i]

    lane128 = lax.broadcasted_iota(jnp.int32, (1, 128), 1)
    low_half = lane128 < HEAD
    q_copy.wait_recv()
    for who in range(2):
        for h in range(HEADS):
            slab = qcomp[who, :, (h // 2) * 128 : (h // 2) * 128 + 128]
            keep = low_half if h % 2 == 0 else jnp.logical_not(low_half)
            slab = jnp.where(keep, slab, jnp.zeros_like(slab))
            for b in range(2):
                qz[h, b * MINE + who * BAND : b * MINE + (who + 1) * BAND, :] = slab[b * BAND : (b + 1) * BAND]

    pass_right(1, 1)
    pass_left(1, 0)
    next_k, next_v = project([(1, 1), (4, 0)])
    first_k = jnp.concatenate([near_k, next_k], axis=0)
    first_v = jnp.concatenate([near_v, next_v], axis=0)
    kt[:, :rest] = first_k[lead : lead + rest].T
    vb[:rest, :CP] = first_v[lead : lead + rest]

    def attend(items, scores_of, values_of, first, between):
        scores = scores_of(*items[0])
        for n, (h, a, b) in enumerate(items):
            following = scores_of(*items[n + 1]) if n + 1 < len(items) else None
            peak = jnp.max(scores, axis=1, keepdims=True)
            if not first:
                old = m_ref[h, a:b][:, :1]
                peak = jnp.maximum(old, peak)
            weights = jnp.exp2(scores - peak).astype(BF16)
            m_ref[h, a:b] = jnp.broadcast_to(peak, (b - a, 128))
            if first:
                acc_ref[h, a:b] = values_of(h, weights)
            else:
                acc_ref[h, a:b] = acc_ref[h, a:b] * jnp.exp2(old - peak) + values_of(h, weights)
            scores = following
            if n in between:
                between[n]()

    def all_heads(a, b):
        return [(h, a, b) for h in range(HEADS)]

    parts = ((0, 0, BAND), (2, BAND, MINE), (1, MINE, MINE + BAND), (2, MINE + BAND, BOTH))

    def own_scores(h, start, stop):
        s = h // 2 * 128
        own = jnp.concatenate([dot(qz[h, a:b], kt3[i, s : s + 128]) for i, a, b in parts], axis=0)
        return jnp.concatenate([own, dot(qz[h, start:stop], kt[s : s + 128, :rest])], axis=1)

    def own_values(h, weights):
        s = h // 2 * 128
        own = jnp.concatenate(
            [
                dot(weights[a:b, :FIRST], jnp.concatenate([v3[i, :, s : s + 128], v3[i, :, CP:]], axis=1))
                for i, a, b in parts
            ],
            axis=0,
        )
        return own + dot(weights[:, FIRST:], jnp.concatenate([vb[:rest, s : s + 128], vb[:rest, CP:]], axis=1))

    def second_first():
        pass_right(2, 0)
        pass_left(2, 1)

    def second_last():
        pass_right(2, 1)
        pass_left(2, 0)

    attend(all_heads(0, BOTH), own_scores, own_values, True, {0: second_first, 2: second_last})

    def chunk(keys, items, between):
        def scores_of(h, a, b):
            s = h // 2 * 128
            return dot(qz[h, a:b], kt[s : s + 128, :keys])

        def values_of(h, weights):
            s = h // 2 * 128
            return dot(weights, jnp.concatenate([vb[:keys, s : s + 128], vb[:keys, CP:]], axis=1))

        attend(items, scores_of, values_of, False, between)

    left_k, left_v = first_k[lead + rest :], first_v[lead + rest :]
    count = left_k.shape[0]
    kb[:count] = left_k
    vb[:count, :CP] = left_v
    k, v = project([(2, 0), (5, 1), (2, 1), (5, 0)])
    kb[count : count + BOTH] = k
    vb[count : count + BOTH, :CP] = v
    count += BOTH
    to_right(3, 0).wait_recv()
    far_right().start()
    to_left(3, 1).wait_recv()
    far_left().start()
    k, v = project([(3, 0), (6, 1)])
    kb[count:] = k[: LONG - count]
    vb[count:, :CP] = v[: LONG - count]
    left_k, left_v = k[LONG - count :], v[LONG - count :]
    kt[...] = kb[...].T
    chunk(LONG, all_heads(0, BOTH), {})

    count = left_k.shape[0]
    kb[:count] = left_k
    vb[:count, :CP] = left_v
    to_right(3, 1).wait_recv()
    to_left(3, 0).wait_recv()
    k, v = project([(3, 1), (6, 0)])
    kb[count : count + MINE] = k
    vb[count : count + MINE, :CP] = v
    count += MINE
    far_right().wait_recv()
    far_left().wait_recv()
    k, v = project([(7, 0), (7, 1)])
    kb[count:LAST] = k
    vb[count:LAST, :CP] = v
    kt[:, :LAST] = kb[:LAST].T

    def merge(b):
        return [
            remote(msend.at[b], mrecv.at[b], mg_send.at[b, 0], mg_recv.at[b, 0], twin),
            remote(nsend.at[b], nrecv.at[b], mg_send.at[b, 1], mg_recv.at[b, 1], twin),
        ]

    def give(b):
        rows = slice(b * MINE + BAND, (b + 1) * MINE)
        notes = jnp.zeros((BAND, 128), F32)
        for h in range(HEADS):
            notes = jnp.where(lane128 == h, m_ref[h, rows], notes)
            notes = jnp.where(lane128 == 8 + h, acc_ref[h, rows, 128:], notes)
        for slab in range(3):
            one = acc_ref[2 * slab, rows, :128]
            if slab < 2:
                one = jnp.where(low_half, one, acc_ref[2 * slab + 1, rows, :128])
            msend[b, :, slab * 128 : (slab + 1) * 128] = one.astype(BF16)
        nsend[b] = notes
        for copy in merge(b):
            copy.start()

    def forward(b, j, source):
        return remote(
            sec.at[b, pl.ds(j * CELLS, CELLS)], xin.at[b, source], f_send.at[b, j], f_recv.at[b, source],
            worker_device(j, z, core),
        )

    def to_self(b):
        return pltpu.make_async_copy(
            sec.at[b, pl.ds(frame * CELLS, CELLS)], xin.at[b, frame], local_sem.at[b]
        )

    def take(b):
        rows = slice(b * MINE, b * MINE + BAND)
        for copy in merge(b):
            copy.wait_recv()
        keep_own, keep_other, sums = [], [], []
        for h in range(HEADS):
            mine, other = m_ref[h, rows], nrecv[b, :, h : h + 1]
            peak = jnp.maximum(mine, other)
            own_part, other_part = jnp.exp2(mine - peak), jnp.exp2(other - peak)
            keep_own.append(own_part)
            keep_other.append(other_part)
            sums.append(
                acc_ref[h, rows, 128:] * own_part + nrecv[b, :, 8 + h : 9 + h] * other_part
            )
        slabs = []
        for slab in range(3):
            e, o = 2 * slab, min(2 * slab + 1, HEADS - 1)

            def pick(values):
                return values[e] if e == o else jnp.where(low_half, values[e], values[o])

            own_sum = pick([acc_ref[h, rows, :128] for h in range(HEADS)])
            joined = own_sum * pick(keep_own) + mrecv[b, :, slab * 128 : (slab + 1) * 128].astype(F32) * pick(keep_other)
            slabs.append((joined / pick(sums)).astype(BF16))
        attended = jnp.concatenate(slabs, axis=1)
        sec[b] = (wide_ref[b * BAND : (b + 1) * BAND].astype(F32) + dot(attended, woutp[...])).astype(BF16)
        for k in range(1, FRAMES):
            j = (frame + k) % FRAMES

            @pl.when(j < WORKERS)
            def _():
                forward(b, j, frame).start()

        @pl.when(frame < WORKERS)
        def _():
            to_self(b).start()

    chunk(LAST, all_heads(0, MINE), {})
    give(0)
    chunk(LAST, all_heads(MINE, BOTH), {1: lambda: take(0)})
    give(1)

    for parity in range(2):
        remote(st_fin, st_own.at[parity], own_send.at[0], own_recv.at[parity], sides[0]).wait_recv()
        factors = [factor_row(ex_ref, parity, r) for r in range(2)]
        columns = rows_of(st_own[parity, 0:1], st_own[parity, 1:2], gain, bias, shift, *factors).T
        mean_c, rstd_c, gain_c, bias_c, shift_c = [columns[:, i : i + 1] for i in range(5)]
        for r in range(2):
            factor_c = columns[:, 5 + r : 6 + r]
            own = lat_ref[parity, r].astype(F32)
            normed_own = ((own - mean_c) * rstd_c * gain_c + bias_c + shift_c).astype(BF16).astype(F32)
            stale_own = code_ref[parity, r].astype(F32) * factor_c
            res_ref[parity, r] = ((normed_own - stale_own) / factor_c).astype(BF16)

    take(1)

    here = x_lo * 4 + y

    def back(b, target):
        return remote(
            yout.at[b, pl.ds(2 * target, 2)],
            out_ref.at[pl.ds(0, 2), pl.ds(frame * CELLS, CELLS)],
            b_send.at[b, target],
            b_recv.at[frame],
            device(target // 4, target % 4, z, b, core),
        )

    @pl.when(frame < WORKERS)
    def _():
        tile = FRAMES * CELLS
        row_cell = lax.broadcasted_iota(jnp.int32, (tile, tile), 0) % CELLS
        col_cell = lax.broadcasted_iota(jnp.int32, (tile, tile), 1) % CELLS
        same = row_cell == col_cell
        for b in range(2):
            for k in range(1, FRAMES):
                forward(b, 0, (frame + k) % FRAMES).wait_recv()
            to_self(b).wait()
            section = xin[b].astype(F32)
            shifted = (section + embed_ref[...][:, None, :]).reshape(tile, C)
            mean = jnp.mean(shifted, axis=-1, keepdims=True)
            deviation = shifted - mean
            normed_t = (
                deviation * lax.rsqrt(jnp.mean(deviation * deviation, axis=-1, keepdims=True) + 1e-05)
            ).astype(BF16)
            proj = dot(normed_t, wp[...]).astype(BF16)
            mixed = []
            for slab in range(3):
                q = proj[:, slab * 128 : (slab + 1) * 128]
                k = proj[:, CP + slab * 128 : CP + (slab + 1) * 128]
                v = proj[:, 2 * CP + slab * 128 : 2 * CP + (slab + 1) * 128]
                halves = []
                for h in range(2 if slab < 2 else 1):
                    keep = low_half if h == 0 else jnp.logical_not(low_half)
                    scores = lax.dot_general(
                        jnp.where(keep, q, jnp.zeros_like(q)), k, (((1,), (1,)), ((), ())),
                        preferred_element_type=F32,
                    ) * (HEAD**-0.5)
                    scores = jnp.where(same, scores, -1e30)
                    weights = jnp.exp(scores - jnp.max(scores, axis=1, keepdims=True))
                    below = jnp.sum(weights, axis=1, keepdims=True)
                    halves.append(dot(weights.astype(BF16), v) / below)
                mixed.append(halves[0] if slab == 2 else jnp.where(low_half, halves[0], halves[1]))
            mix = jnp.concatenate(mixed, axis=1).astype(BF16)
            result = section.reshape(tile, C) + dot(mix, wtoutp[...])
            yout[b] = result.astype(BF16).reshape(FRAMES, CELLS, C)
            for k in range(8):
                stays = jnp.logical_and(k == 0, x_hi == b)

                @pl.when(stays)
                def _():
                    pltpu.make_async_copy(
                        yout.at[b, pl.ds(2 * here, 2)],
                        out_ref.at[pl.ds(0, 2), pl.ds(frame * CELLS, CELLS)],
                        local_sem.at[2],
                    ).start()

                @pl.when(jnp.logical_not(stays))
                def _():
                    back(b, (here + k) % 8).start()

    for s in range(WORKERS):

        @pl.when(frame == s)
        def _():
            pltpu.make_async_copy(
                yout.at[0, pl.ds(0, 2)], out_ref.at[pl.ds(0, 2), pl.ds(s * CELLS, CELLS)], local_sem.at[2]
            ).wait()

        @pl.when(frame != s)
        def _():
            remote(
                yout.at[0, pl.ds(0, 2)], out_ref.at[pl.ds(0, 2), pl.ds(s * CELLS, CELLS)],
                b_send.at[0, 0], b_recv.at[s], twin,
            ).wait_recv()

    for parity in range(2):
        for send in (side_copy, lat_copy):
            send(parity, x_hi).wait_send()
        for piece in range(2):
            code_copy(parity, x_hi, piece).wait_send()
    for copy in all_copies + own_copies:
        copy.wait_send()
    q_copy.wait_send()
    for step in range(1, 4):
        for b in range(2):
            to_right(step, b).wait_send()
            to_left(step, b).wait_send()
    far_right().wait_send()
    far_left().wait_send()
    for b in range(2):
        for copy in merge(b):
            copy.wait_send()
        for k in range(1, FRAMES):
            j = (frame + k) % FRAMES

            @pl.when(j < WORKERS)
            def _():
                forward(b, j, frame).wait_send()

    @pl.when(frame < WORKERS)
    def _():
        for b in range(2):
            for k in range(8):

                @pl.when(jnp.logical_not(jnp.logical_and(k == 0, x_hi == b)))
                def _():
                    back(b, (here + k) % 8).wait_send()


def frame_table():
    half = C // 2
    frequency = np.exp(-math.log(10000.0) * np.arange(half) / half)
    angles = np.arange(FRAMES)[:, None] * frequency
    return np.concatenate([np.cos(angles), np.sin(angles)], axis=-1).astype(np.float32)


VM = pl.BlockSpec(memory_space=pltpu.VMEM)
SM = pl.BlockSpec(memory_space=pltpu.SMEM)
HBM = pl.BlockSpec(memory_space=pl.ANY)


def body(
    latent, timestep, time_weight, norm_gain, norm_bias, spatial_qkv, spatial_out,
    stale_codes, stale_exponents, temporal_qkv, temporal_out,
):
    dma = pltpu.SemaphoreType.DMA
    output, residual = pl.pallas_call(
        kernel,
        out_shape=(pltpu.VMEM((2, BAND, C), BF16), pltpu.VMEM((2, 2, C, W), BF16)),
        in_specs=[SM, SM] + [VM] * 5 + [HBM] * 5,
        out_specs=(VM, VM),
        scratch_shapes=[
            pltpu.VMEM((C, C), BF16),
            pltpu.VMEM((C, 3 * C), BF16),
            pltpu.VMEM((C, C), BF16),
            pltpu.VMEM((C, 3 * C), BF16),
            pltpu.VMEM((C, C), BF16),
            pltpu.VMEM((2, 2, C, W), BF16),
            pltpu.VMEM((MINE, C), BF16),
            pltpu.VMEM((2, PACK, 128), BF16),
            pltpu.VMEM((ZS, 2, PACK, 128), BF16),
            pltpu.VMEM((8, C), F32),
            pltpu.VMEM((2, 8, C), F32),
            pltpu.VMEM((2, 8, C), F32),
            pltpu.VMEM((2 * ZS, 8, C), F32),
            pltpu.VMEM((8, C), F32),
            pltpu.VMEM((2, 8, C), F32),
            pltpu.VMEM((256, 2 * CP), BF16),
            pltpu.VMEM((128, 2 * CP), BF16),
            pltpu.VMEM((128, 2 * CP), BF16),
            pltpu.VMEM((C, CP), BF16),
            pltpu.VMEM((CP, C), BF16),
            pltpu.VMEM((C, 3 * CP), BF16),
            pltpu.VMEM((CP, C), BF16),
            pltpu.VMEM((2, MINE, CP), BF16),
            pltpu.VMEM((HEADS, BOTH, 128), BF16),
            pltpu.VMEM((LONG, CP), BF16),
            pltpu.VMEM((CP, LONG), BF16),
            pltpu.VMEM((LONG, 512), BF16),
            pltpu.VMEM((3, CP, FIRST), BF16),
            pltpu.VMEM((3, FIRST, 512), BF16),
            pltpu.VMEM((HEADS, BOTH, 128), F32),
            pltpu.VMEM((HEADS, BOTH, 256), F32),
            pltpu.VMEM((2, BAND, CP), BF16),
            pltpu.VMEM((2, BAND, CP), BF16),
            pltpu.VMEM((2, BAND, 128), F32),
            pltpu.VMEM((2, BAND, 128), F32),
            pltpu.VMEM((2, BAND, C), BF16),
            pltpu.VMEM((2, FRAMES, CELLS, C), BF16),
            pltpu.VMEM((2, FRAMES, CELLS, C), BF16),
            pltpu.VMEM((C, C), BF16),
            dma((5,)), dma((2,)), dma((2,)), dma((2, 2)), dma((2, 2)), dma((7,)), dma((7,)), dma((7,)), dma((7,)),
            dma((2,)), dma((2,)), dma((2 * ZS,)), dma((2 * ZS,)), dma((2,)), dma((2,)), dma((2,)),
            dma((2, 2)), dma((2, 2)),
            dma((2, FRAMES)), dma((2, FRAMES)), dma((2, 8)), dma((WORKERS,)), dma((3,)),
        ],
        compiler_params=pltpu.CompilerParams(
            collective_id=0, has_side_effects=True, vmem_limit_bytes=60 * 2**20
        ),
        name="block",
    )(
        timestep, stale_exponents, jnp.transpose(latent, (0, 1, 3, 2)), jnp.transpose(stale_codes, (0, 1, 3, 2)),
        norm_gain, norm_bias, jnp.asarray(frame_table()),
        time_weight, spatial_qkv, spatial_out, temporal_qkv, temporal_out,
    )
    return output.reshape(2, 2, W, C), jnp.transpose(residual, (0, 1, 3, 2))


def solution(mesh):
    placed = (
        P("frame", "patch", None, None),
        P(),
        P(),
        P(),
        P(),
        P(),
        P(),
        P("frame", "patch", None, None),
        P("frame", "patch", None),
        P(),
        P(),
    )
    return jax.shard_map(
        body,
        mesh=mesh,
        in_specs=placed,
        out_specs=(P("frame", "patch", None, None), P("frame", "patch", None, None)),
        check_vma=False,
    )
```
